32 devices in a mesh: site: 2 (over x), var: 8 (over z, y), sub: 2 (over core).
Axes of the slice: x: 2, y: 2, z: 4, core: 2. Of those that a mesh axis runs over, the one named last changes fastest.
Arguments:
- fault_points: float32 [2, 1024], P(None, 'site'), parts along dimension 1, may hold values from 0 to 40
- hypocenter: int32 [16384], P(('site', 'var')), parts along dimension 0, may hold values from 0 to 511
- velocity: float32 [16384], P(('site', 'var')), parts along dimension 0, may hold values from 2 to 3.5
- rise_time: float32 [16384], P(('site', 'var')), parts along dimension 0, may hold values from 0.2 to 1
- member_mask: int32 [16384, 512], P(('site', 'var'), 'sub'), parts along dimension 0, may hold values 0 or 1
- slip_amount: float32 [16384, 512], P(('site', 'var'), 'sub'), parts along dimension 0, may hold values from 0.3 to 3
- moment_tensor: float32 [6, 1024], P(None, ('site', 'sub')), parts along dimension 1, may hold values from -6 to 6
- strain_green: bfloat16 [4, 6, 2, 256, 16, 128], P('site', None, 'sub', 'var'), parts along dimension 0, may hold values from -0.109375 to 0.109375
- station_ids: int32 [256], P('site'), parts along dimension 0, may hold values from 0 to 127, each once
Outputs:
- spectra: float32 [16, 2, 128, 16384], P(None, None, 'sub', ('site', 'var')), parts along dimension 3
The draws below stay inside these ranges and needn't reach their ends.
There are 2 independent parts, one for each index of `site`. The reference program is written for one: setup_inputs(seed, part) draws one part's arguments, and reference() takes and returns one part's arrays. A program takes and returns all parts, laid end to end along the dimension named above; each array names one. Nothing has to cross between parts.
Inputs may be any that keep to these rules, and one draw needn't show every extreme that they name: `station_ids`: each station once.
All inputs are finite; a program needn't handle non-finite values. No bound on the sum of `member_mask` on one device may be relied on, other than what follows from the above.
Results may differ from the reference program's by a relative error of at most 0.0041.
Values may be sent and summed in bfloat16 or wider, within the bound.
No kernel may reach another device: no remote copies, remote signals or barrier semaphores. Data moves between devices by JAX's collectives and lax.ppermute only.
A program may use at most 192 MiB of HBM per device.

```python
import math
import jax
import jax.numpy as jnp
from jax import lax

MS = 256
NF = 16
NS = 128
V = 8192
M = 512
N_SUB = 2


def plant(drawn, rng, low, high):
    extent = drawn.shape
    index_at = [jax.random.randint(jax.random.fold_in(rng, axis), (), 0, extent[axis]) for axis in range(len(extent))]
    drawn = drawn.at[tuple(index_at)].set(low)
    longest = extent.index(max(extent))
    index_at[longest] = (index_at[longest] + 1) % extent[longest]
    return drawn.at[tuple(index_at)].set(high)


def level_of(own_key, dims, pieces, low, largest):
    level = 1.0
    for position, parts in pieces:
        steps = jax.random.uniform(jax.random.fold_in(jax.random.fold_in(own_key, 6), position), (parts,), jnp.float32, low / len(pieces), largest / len(pieces))
        level = level * jnp.repeat(jnp.exp(steps), dims[position] // parts).reshape((-1,) + (1,) * (len(dims) - 1 - position))
    return level


def bell_draw(rng, dims, spread, most, pieces=(), held_as=jnp.bfloat16):
    array = jax.random.normal(rng, dims, jnp.float32) * spread
    if len(pieces) > 0:
        array = level_of(rng, dims, pieces, -0.22, 0.18) * array
    return jnp.clip(array, min=-most, max=most).astype(held_as)


def setup_inputs(seed: int = 0, part: int = 0) -> dict:
    splits = jax.random.split(jax.random.key(seed), 10)
    part_keys = jax.random.split(jax.random.fold_in(splits[9], part), 10)
    fault_points = jnp.clip(jax.random.uniform(part_keys[0], (2, M), jnp.float32, 0.0, 40.0), 0.0, 40.0)
    hypocenter = plant(jax.random.randint(part_keys[1], (V,), 0, M), jax.random.fold_in(part_keys[1], 1), 0, M - 1).astype(jnp.int32)
    velocity = jnp.clip(2.0 + 1.5 * jax.random.uniform(part_keys[2], (V,), jnp.float32) ** level_of(part_keys[2], (V,), ((0, 8),), -0.2, 0.2), 2.0, 3.5)
    rise_time = jnp.clip(jnp.exp(math.log(1.0) - 1.609438 * jax.random.uniform(part_keys[3], (V,), jnp.float32) ** level_of(part_keys[3], (V,), ((0, 8),), -0.2, 0.2)), 0.2, 1.0)
    member_mask = plant((jax.random.randint(part_keys[4], (V, M), 0, 4) < 3).astype(jnp.int32), jax.random.fold_in(part_keys[4], 1), 0, 1)
    slip_amount = jnp.clip(jnp.exp(math.log(3.0) - 2.3025851 * jax.random.uniform(part_keys[5], (V, M), jnp.float32) ** level_of(part_keys[5], (V, M), ((0, 8), (1, 2)), -0.2, 0.2)), 0.3, 3.0)
    moment_tensor = bell_draw(part_keys[6], (6, M), 1.0, 6.0, ((1, 2),), jnp.float32)
    strain_green = bell_draw(part_keys[7], (2, 6, N_SUB, MS, NF, NS), (6 * M) ** -0.5, 0.109375, ((2, 2), (3, 8)))
    station_ids = jax.random.permutation(part_keys[8], NS).astype(jnp.int32)
    return dict(fault_points=fault_points, hypocenter=hypocenter, velocity=velocity, rise_time=rise_time, member_mask=member_mask, slip_amount=slip_amount, moment_tensor=moment_tensor, strain_green=strain_green, station_ids=station_ids)


def rotate(green, tensor, station_ids):
    total = green[:, 0].astype(jnp.float32) * tensor[0][None, :, None, None]
    for comp in range(1, 6):
        total = total + green[:, comp].astype(jnp.float32) * tensor[comp][None, :, None, None]
    return jnp.take(total, station_ids, axis=3).astype(jnp.bfloat16)

def reference(fault_points, hypocenter, velocity, rise_time, member_mask, slip_amount, moment_tensor, strain_green, station_ids):
    green = strain_green.reshape((2, 6, M, NF, NS))
    rotated = rotate(green, moment_tensor, station_ids)
    upper = jnp.concatenate([rotated[0], rotated[1]], axis=2)
    lower = jnp.concatenate([-rotated[1], rotated[0]], axis=2)
    blocks = jnp.concatenate([upper, lower], axis=0)
    blocks = jnp.transpose(blocks, (1, 0, 2))
    focus = jnp.take(fault_points, hypocenter, axis=1)
    east_gap = fault_points[0][None, :] - focus[0][:, None]
    north_gap = fault_points[1][None, :] - focus[1][:, None]
    delay = jnp.sqrt(east_gap * east_gap + north_gap * north_gap) / velocity[:, None]
    amount = member_mask.astype(jnp.float32) * slip_amount
    omega = (jnp.arange(NF, dtype=jnp.int32) + 1).astype(jnp.float32) * (2.0 * math.pi * 0.0625)

    def at_freq(inputs):
        pulsation, block = inputs
        phase = pulsation * delay
        damping = (pulsation * rise_time)[:, None]
        scale = amount / (1.0 + damping * damping)
        cosine = jnp.cos(phase)
        sine = jnp.sin(phase)
        real = scale * (cosine - damping * sine)
        imag = -scale * (sine + damping * cosine)
        slips = jnp.concatenate([real, imag], axis=1).astype(jnp.bfloat16)
        slips = lax.optimization_barrier(slips).astype(jnp.float32)
        out = jnp.dot(block.astype(jnp.float32).T, slips.T)
        return out.reshape((2, NS, V))
    return lax.map(at_freq, (omega, blocks))
```

```python
import functools

import jax
import jax.numpy as jnp
from jax import lax
from jax.experimental import pallas as pl
from jax.experimental.pallas import tpu as pltpu
from jax.sharding import PartitionSpec as P

VMEM = pl.BlockSpec(memory_space=pltpu.VMEM)
SMEM = pl.BlockSpec(memory_space=pltpu.SMEM)
ANY = pl.BlockSpec(memory_space=pl.ANY)
PARAMS = pltpu.CompilerParams(vmem_limit_bytes=56 * 2**20)
BASE_FREQ = 0.0625
LANES = 256


def rotate_kernel(green_ref, tensor_ref, ids_ref, own_ref, other_ref, sums, rows):
    _, comps, count, freqs, stations = green_ref.shape
    half = stations // 2
    first = lax.axis_index("var") * count

    def one_subfault(m, carry):
        for part in range(2):
            total = green_ref[part, 0, m].astype(jnp.float32) * tensor_ref[0, first + m]
            for comp in range(1, comps):
                total = total + green_ref[part, comp, m].astype(jnp.float32) * tensor_ref[comp, first + m]
            at = pl.ds(pl.multiple_of(m * freqs, freqs), freqs)
            sums[at, part * stations : (part + 1) * stations] = total.astype(jnp.bfloat16)
        return carry

    lax.fori_loop(0, count, one_subfault, 0, unroll=4)

    lane = lax.broadcasted_iota(jnp.int32, (1, stations), 1)
    ids = ids_ref[...]
    turned = pltpu.roll(ids, half, 1)
    low = jnp.where(lane < half, ids, turned)
    high = jnp.where(lane < half, turned, ids)
    is_first = lax.axis_index("sub") == 0
    wanted = jnp.concatenate([jnp.where(is_first, low, high), jnp.where(is_first, high, low)], axis=1)
    row = lax.broadcasted_iota(jnp.int32, (2 * stations, 2 * stations), 0)
    column = lax.broadcasted_iota(jnp.int32, (2 * stations, 2 * stations), 1)
    part_of_column = (column // half) % 2
    picks = (row == wanted + part_of_column * stations).astype(jnp.float32).astype(jnp.bfloat16)
    picked = jnp.dot(sums[...], picks, preferred_element_type=jnp.float32)
    rows[0] = picked[:, :stations]
    rows[1] = picked[:, stations:]
    for k in range(freqs):
        at = pl.ds(k, count, stride=freqs)
        own_ref[k] = rows[0, at, :].astype(jnp.bfloat16)
        other_ref[k] = rows[1, at, :].astype(jnp.bfloat16)


def rotate(green, tensor, station_ids):
    _, _, count, freqs, stations = green.shape
    piece = jax.ShapeDtypeStruct((freqs, count, stations), jnp.bfloat16)
    return pl.pallas_call(
        rotate_kernel,
        out_shape=(piece, piece),
        in_specs=[VMEM, SMEM, VMEM],
        out_specs=(VMEM, VMEM),
        scratch_shapes=[
            pltpu.VMEM((count * freqs, 2 * stations), jnp.bfloat16),
            pltpu.VMEM((2, count * freqs, stations), jnp.float32),
        ],
        compiler_params=PARAMS,
        name="rotate",
    )(green, tensor, station_ids.reshape((1, stations)))


def amount_kernel(mask_ref, slip_ref, out_ref):
    out_ref[...] = (mask_ref[...].astype(jnp.float32) * slip_ref[...]).T


def amounts(mask, slip):
    variations, subfaults = mask.shape
    block = pl.BlockSpec((LANES, subfaults), lambda i: (i, 0))
    return pl.pallas_call(
        amount_kernel,
        out_shape=jax.ShapeDtypeStruct((subfaults, variations), jnp.float32),
        grid=(variations // LANES,),
        in_specs=[block, block],
        out_specs=pl.BlockSpec((subfaults, LANES), lambda i: (0, i)),
        compiler_params=PARAMS,
        name="amounts",
    )(mask, slip)


SIN = (3.14159264, -5.16771008, 2.55007751, -0.598291190, 0.0776574420)
COS = (0.999999953, -4.93479283, 4.05841131, -1.33187624, 0.219688854)


def sine_cosine(turns):
    rest = turns - jnp.floor(turns + 0.5)
    square = rest * rest
    sine = SIN[-1]
    for c in SIN[-2::-1]:
        sine = sine * square + c
    sine = sine * rest
    cosine = COS[-1]
    for c in COS[-2::-1]:
        cosine = cosine * square + c
    return 2.0 * sine * cosine, 1.0 - 2.0 * sine * sine


def spectra_kernel(
    first, count, pieces, steps, off_ref, points_ref, focus_ref, velocity_ref, rise_ref, own_ref, other_ref, *refs
):
    piece_refs = refs[:pieces]
    out_ref, rotated, columns = refs[-5], refs[-4], refs[-3]
    slots = (refs[-2], refs[-1])
    half = own_ref.shape[0]
    step = pl.program_id(0)
    chunk = 32
    loops = 2 * half // (2 * chunk)

    @pl.when(step == 0)
    def _():
        for piece, ref in enumerate(piece_refs):
            rows = ref.shape[1] // 2
            at = pl.multiple_of(off_ref[piece], 32)
            rotated[:, pl.ds(at, rows), :] = ref[:, :rows, :]
            rotated[:, pl.ds(half + at, rows), :] = ref[:, rows:, :]
        for axis in range(2):
            wide = jnp.broadcast_to(points_ref[axis : axis + 1, :], (128, 2 * half))
            columns[axis] = wide.T

    def slips_of(row, lanes, source, source_row, slot):
        at = pl.ds(row, chunk)
        east = columns[0, at, :] - focus_ref[0:1, lanes]
        north = columns[1, at, :] - focus_ref[1:2, lanes]
        gap = east * east + north * north
        distance = gap * lax.rsqrt(jnp.maximum(gap, 1e-30))
        turns = distance * (BASE_FREQ / velocity_ref[0:1, lanes])
        sine, cosine = sine_cosine(turns)
        amount = source[pl.ds(source_row, chunk), lanes]
        twice = 2.0 * cosine
        re_last, im_last = amount, None
        re, im = amount * cosine, amount * sine
        for k in range(first + count):
            if k >= first:
                slot[0, k - first, at, lanes] = re.astype(jnp.bfloat16)
                slot[1, k - first, at, lanes] = im.astype(jnp.bfloat16)
            re, re_last = twice * re - re_last, re
            im, im_last = (twice * im if im_last is None else twice * im - im_last), im

    def sums_of(k, slot):
        dims = (((0,), (0,)), ((), ()))
        by_re = lax.dot_general(rotated[k], slot[0, k], dims, preferred_element_type=jnp.float32)
        by_im = lax.dot_general(rotated[k], slot[1, k], dims, preferred_element_type=jnp.float32)
        stations = by_re.shape[0] // 2
        re = by_re[:stations] + by_im[stations:]
        im = by_re[stations:] - by_im[:stations]
        pulsation = (first + k + 1).astype(jnp.float32) * (2.0 * jnp.pi * BASE_FREQ)
        damping = pulsation * rise_ref[0:1, :]
        scale = 1.0 / (1.0 + damping * damping)
        tilt = scale * damping
        out_ref[k, 0] = scale * re + tilt * im
        out_ref[k, 1] = scale * im - tilt * re

    def run(fill, drain):
        def body(j, carry):
            if fill is not None:
                for lane in range(0, LANES, 128):
                    lanes = slice(lane, lane + 128)
                    row = pl.multiple_of(j * chunk, chunk)
                    slips_of(row, lanes, own_ref, row, fill)
                    slips_of(pl.multiple_of(half + j * chunk, chunk), lanes, other_ref, row, fill)
            if drain is not None:
                for k in range(count // loops):
                    sums_of(j * (count // loops) + k, drain)
            return carry

        lax.fori_loop(0, loops, body, 0)

    for i in range(steps + 1):
        pl.when(step == i)(
            functools.partial(run, slots[i % 2] if i < steps else None, slots[(i + 1) % 2] if i > 0 else None)
        )


def spectra(first, count, total, offsets, points, focus, velocity, rise_time, own, other, pieces, so_far):
    half, variations = own.shape
    steps = variations // LANES
    stations = pieces[0].shape[2] // 2
    fill = lambda i: jnp.minimum(i, steps - 1)
    drain = lambda i: jnp.maximum(i - 1, 0)
    row = pl.BlockSpec((1, LANES), lambda i: (0, fill(i)))
    args = [offsets, points, focus, velocity, rise_time, own, other, *pieces]
    specs = [
        SMEM,
        VMEM,
        pl.BlockSpec((2, LANES), lambda i: (0, fill(i))),
        row,
        pl.BlockSpec((1, LANES), lambda i: (0, drain(i))),
        pl.BlockSpec((half, LANES), lambda i: (0, fill(i))),
        pl.BlockSpec((half, LANES), lambda i: (0, fill(i))),
    ]
    for piece in pieces:
        at = first // count if piece.shape[0] == total else 0
        specs.append(pl.BlockSpec((count,) + piece.shape[1:], lambda i, at=at: (at, 0, 0)))
    aliases = {}
    if so_far is not None:
        aliases = {len(args): 0}
        args.append(so_far)
        specs.append(ANY)
    slot = pltpu.VMEM((2, count, 2 * half, LANES), jnp.bfloat16)
    return pl.pallas_call(
        functools.partial(spectra_kernel, first, count, len(pieces), steps),
        out_shape=jax.ShapeDtypeStruct((total, 2, stations, variations), jnp.float32),
        grid=(steps + 1,),
        in_specs=specs,
        out_specs=pl.BlockSpec((count, 2, stations, LANES), lambda i: (first // count, 0, 0, drain(i))),
        scratch_shapes=[
            pltpu.VMEM((count, 2 * half, 2 * stations), jnp.bfloat16),
            pltpu.VMEM((2, 2 * half, 128), jnp.float32),
            slot,
            slot,
        ],
        input_output_aliases=aliases,
        compiler_params=PARAMS,
        name="spectra",
    )(*args)


def swap(array, axis):
    return lax.ppermute(array, axis, [(0, 1), (1, 0)])


def gather(own, received, size):
    place = lax.axis_index("var")
    rows = own.shape[1]
    if size != 8:
        whole = [lax.all_gather(piece, "var", axis=1, tiled=True) for piece in (own, received)]
        return [jnp.concatenate(whole, axis=1)], jnp.zeros((1,), jnp.int32)
    block = jnp.concatenate([own, received], axis=1)
    along = lambda piece, s: lax.ppermute(piece, "var", [(i, (i + 2 * s) % 8) for i in range(8)])
    across = lambda piece: lax.ppermute(piece, "var", [(i, i ^ 1) for i in range(8)])
    pieces = [block] + [along(block, s) for s in (1, 3, 2)]
    pieces += [across(piece) for piece in pieces]
    source = [((place - 2 * s) % 8) ^ flip for flip in (0, 1) for s in (0, 1, 3, 2)]
    return pieces, jnp.stack(source).astype(jnp.int32) * rows


def shards(size, fault_points, hypocenter, velocity, rise_time, member_mask, slip_amount, moment_tensor, strain_green, station_ids):
    half = moment_tensor.shape[1]
    freqs = strain_green.shape[4]
    own_part, other_part = rotate(strain_green[:, :, 0], moment_tensor, station_ids)
    pieces, offsets = gather(own_part, swap(other_part, "sub"), size)
    own = amounts(member_mask, slip_amount)
    other = swap(own, "sub")
    focus = jnp.take(fault_points, hypocenter, axis=1)
    turned = jnp.concatenate([fault_points[:, half:], fault_points[:, :half]], axis=1)
    points = jnp.where(lax.axis_index("sub") == 0, fault_points, turned)
    rows = (velocity[None, :], rise_time[None, :])
    out = None
    for first in (0, freqs // 2):
        out = spectra(first, freqs // 2, freqs, offsets, points, focus, *rows, own, other, pieces, out)
    return out


def solution(mesh):
    placed = (
        P(None, "site"),
        P(("site", "var")),
        P(("site", "var")),
        P(("site", "var")),
        P(("site", "var"), "sub"),
        P(("site", "var"), "sub"),
        P(None, ("site", "sub")),
        P("site", None, "sub", "var", None, None),
        P("site"),
    )
    return jax.shard_map(
        functools.partial(shards, mesh.shape["var"]),
        mesh=mesh,
        in_specs=placed,
        out_specs=P(None, None, "sub", ("site", "var")),
        check_vma=False,
    )
```

```python
import functools

import jax
import jax.numpy as jnp
from jax import lax
from jax.experimental import pallas as pl
from jax.experimental.pallas import tpu as pltpu
from jax.sharding import PartitionSpec as P

VMEM = pl.BlockSpec(memory_space=pltpu.VMEM)
SMEM = pl.BlockSpec(memory_space=pltpu.SMEM)
ANY = pl.BlockSpec(memory_space=pl.ANY)
PARAMS = pltpu.CompilerParams(vmem_limit_bytes=12 * 2**20)
BASE_FREQ = 0.0625
LANES = 256


def rotate_kernel(green_ref, tensor_ref, ids_ref, own_ref, other_ref, sums, rows):
    _, comps, count, freqs, stations = green_ref.shape
    half = stations // 2
    first = lax.axis_index("var") * count

    def one_subfault(m, carry):
        for part in range(2):
            total = green_ref[part, 0, m].astype(jnp.float32) * tensor_ref[0, first + m]
            for comp in range(1, comps):
                total = total + green_ref[part, comp, m].astype(jnp.float32) * tensor_ref[comp, first + m]
            at = pl.ds(pl.multiple_of(m * freqs, freqs), freqs)
            sums[at, part * stations : (part + 1) * stations] = total.astype(jnp.bfloat16)
        return carry

    lax.fori_loop(0, count, one_subfault, 0, unroll=4)

    lane = lax.broadcasted_iota(jnp.int32, (1, stations), 1)
    ids = ids_ref[...]
    turned = pltpu.roll(ids, half, 1)
    low = jnp.where(lane < half, ids, turned)
    high = jnp.where(lane < half, turned, ids)
    is_first = lax.axis_index("sub") == 0
    wanted = jnp.concatenate([jnp.where(is_first, low, high), jnp.where(is_first, high, low)], axis=1)
    row = lax.broadcasted_iota(jnp.int32, (2 * stations, 2 * stations), 0)
    column = lax.broadcasted_iota(jnp.int32, (2 * stations, 2 * stations), 1)
    part_of_column = (column // half) % 2
    picks = (row == wanted + part_of_column * stations).astype(jnp.float32).astype(jnp.bfloat16)
    picked = jnp.dot(sums[...], picks, preferred_element_type=jnp.float32)
    rows[0] = picked[:, :stations]
    rows[1] = picked[:, stations:]
    for k in range(freqs):
        at = pl.ds(k, count, stride=freqs)
        own_ref[k] = rows[0, at, :].astype(jnp.bfloat16)
        other_ref[k] = rows[1, at, :].astype(jnp.bfloat16)


def rotate(green, tensor, station_ids):
    _, _, count, freqs, stations = green.shape
    piece = jax.ShapeDtypeStruct((freqs, count, stations), jnp.bfloat16)
    return pl.pallas_call(
        rotate_kernel,
        out_shape=(piece, piece),
        in_specs=[VMEM, SMEM, VMEM],
        out_specs=(VMEM, VMEM),
        scratch_shapes=[
            pltpu.VMEM((count * freqs, 2 * stations), jnp.bfloat16),
            pltpu.VMEM((2, count * freqs, stations), jnp.float32),
        ],
        compiler_params=PARAMS,
        name="rotate",
    )(green, tensor, station_ids.reshape((1, stations)))


def amount_kernel(mask_ref, slip_ref, out_ref):
    out_ref[...] = (mask_ref[...].astype(jnp.float32) * slip_ref[...]).T


def amounts(mask, slip):
    variations, subfaults = mask.shape
    block = pl.BlockSpec((LANES, subfaults), lambda i: (i, 0))
    return pl.pallas_call(
        amount_kernel,
        out_shape=jax.ShapeDtypeStruct((subfaults, variations), jnp.float32),
        grid=(variations // LANES,),
        in_specs=[block, block],
        out_specs=pl.BlockSpec((subfaults, LANES), lambda i: (0, i)),
        compiler_params=PARAMS,
        name="amounts",
    )(mask, slip)


SIN = (3.14159264, -5.16771008, 2.55007751, -0.598291190, 0.0776574420)
COS = (0.999999953, -4.93479283, 4.05841131, -1.33187624, 0.219688854)


def sine_cosine(turns):
    rest = turns - jnp.floor(turns + 0.5)
    square = rest * rest
    sine = SIN[-1]
    for c in SIN[-2::-1]:
        sine = sine * square + c
    sine = sine * rest
    cosine = COS[-1]
    for c in COS[-2::-1]:
        cosine = cosine * square + c
    return 2.0 * sine * cosine, 1.0 - 2.0 * sine * sine


def slips_kernel(chunk, rows, sub, points_ref, hypocenter_ref, velocity_ref, own_ref, other_ref, *refs):
    outs, columns, spots = refs[:-2], refs[-2], refs[-1]
    half, variations = own_ref.shape
    subfaults = 2 * half
    first = pl.multiple_of(lax.axis_index(sub) * half, half)
    second = pl.multiple_of(half - first, half)
    for axis in range(2):
        for at, start in ((0, first), (half, second)):
            wide = jnp.broadcast_to(points_ref[axis : axis + 1, pl.ds(start, half)], (128, half))
            columns[axis, at : at + half, :] = wide.T

    rest = points_ref[...]
    thirds = []
    for _ in range(3):
        thirds.append(rest.astype(jnp.bfloat16))
        rest = rest - thirds[-1].astype(jnp.float32)
    thirds = jnp.concatenate([t.astype(jnp.float32) for t in thirds], axis=0).astype(jnp.bfloat16)
    for lane in range(0, variations, LANES):
        lanes = slice(lane, lane + LANES)
        index = lax.broadcasted_iota(jnp.int32, (subfaults, LANES), 0)
        here = (index == hypocenter_ref[0:1, lanes]).astype(jnp.float32).astype(jnp.bfloat16)
        spot = jnp.dot(thirds, here, preferred_element_type=jnp.float32)
        spots[0:2, lanes] = (spot[0:2] + spot[2:4]) + spot[4:6]
        spots[2:3, lanes] = BASE_FREQ / velocity_ref[0:1, lanes]

    def fill(row, source, source_row, place, lanes):
        at = pl.ds(row, chunk)
        east = columns[0, at, :] - spots[0:1, lanes]
        north = columns[1, at, :] - spots[1:2, lanes]
        gap = east * east + north * north
        distance = gap * lax.rsqrt(jnp.maximum(gap, 1e-30))
        sine, cosine = sine_cosine(distance * spots[2:3, lanes])
        amount = source[pl.ds(source_row, chunk), lanes]
        twice = 2.0 * cosine
        re_last, im_last = amount, None
        re, im = amount * cosine, amount * sine
        for out in outs:
            for k in range(out.shape[0]):
                out[k, pl.ds(place, chunk), lanes] = re.astype(jnp.bfloat16)
                out[k, pl.ds(place + 2 * rows, chunk), lanes] = im.astype(jnp.bfloat16)
                re, re_last = twice * re - re_last, re
                im, im_last = (twice * im if im_last is None else twice * im - im_last), im

    def body(j, carry):
        row = pl.multiple_of(j * chunk, chunk)
        place = pl.multiple_of((row // rows) * (4 * rows) + row % rows, chunk)
        for lane in range(0, variations, 128):
            lanes = slice(lane, lane + 128)
            fill(row, own_ref, row, place, lanes)
            fill(half + row, other_ref, row, pl.multiple_of(place + rows, chunk), lanes)
        return carry

    lax.fori_loop(0, half // chunk, body, 0)


def slips(groups, rows, points, hypocenter, velocity, own, other):
    half, variations = own.shape
    return pl.pallas_call(
        functools.partial(slips_kernel, 32, rows, "sub"),
        out_shape=tuple(jax.ShapeDtypeStruct((n, 4 * half, variations), jnp.bfloat16) for n in groups),
        in_specs=[VMEM] * 5,
        out_specs=(VMEM,) * len(groups),
        scratch_shapes=[pltpu.VMEM((2, 2 * half, 128), jnp.float32), pltpu.VMEM((8, variations), jnp.float32)],
        compiler_params=PARAMS,
        name="slips",
    )(points, hypocenter[None, :], velocity[None, :], own, other)


def unit_rows(k, pair, flip, table):
    lane = lax.broadcasted_iota(jnp.int32, (1, pair[0].shape[2]), 1)
    half = pair[0].shape[2] // 2
    rows = pair[0].shape[1]
    for i, ref in enumerate(pair):
        at = pl.multiple_of((i ^ flip) * (2 * rows), 2 * rows) if len(pair) == 2 else 0
        block = ref[k]
        turned = pltpu.roll(block.astype(jnp.float32), half, 1)
        table[pl.ds(at, rows), :] = block
        table[pl.ds(at + rows, rows), :] = jnp.where(lane < half, turned, -turned).astype(jnp.bfloat16)


def unit_sum(k, slip_k, unit, pair, slips_ref, flip, table):
    unit_rows(k, pair, flip, table)
    depth = table.shape[0]
    at = pl.multiple_of(unit * depth, depth)
    return lax.dot_general(
        table[...], slips_ref[slip_k, pl.ds(at, depth), :], (((0,), (0,)), ((), ())), preferred_element_type=jnp.float32
    )


def partial_kernel(units, width, numbers_ref, *refs):
    pairs = [refs[i * width : (i + 1) * width] for i in range(units)]
    rest = refs[units * width :]
    groups = (len(rest) - 1) // 2
    slip_refs, out_refs, tables = rest[:groups], rest[groups : 2 * groups], rest[-1]
    flip = numbers_ref[0]
    first = 0
    for slips_ref, out_ref in zip(slip_refs, out_refs):

        def body(k, carry, slips_ref=slips_ref, out_ref=out_ref, first=first):
            total = 0.0
            for u in range(units):
                total += unit_sum(first + k, k, numbers_ref[1 + u], pairs[u], slips_ref, flip, tables.at[u])
            out_ref[k] = total
            return carry

        lax.fori_loop(0, slips_ref.shape[0], body, 0)
        first += slips_ref.shape[0]


def partial_sums(numbers, pairs, slip_groups):
    width = len(pairs[0])
    rows = pairs[0][0].shape[1]
    lanes = pairs[0][0].shape[2]
    variations = slip_groups[0].shape[2]
    flat = [piece for pair in pairs for piece in pair]
    return pl.pallas_call(
        functools.partial(partial_kernel, len(pairs), width),
        out_shape=tuple(jax.ShapeDtypeStruct((g.shape[0], lanes, variations), jnp.float32) for g in slip_groups),
        in_specs=[SMEM] + [VMEM] * (len(flat) + len(slip_groups)),
        out_specs=(VMEM,) * len(slip_groups),
        scratch_shapes=[pltpu.VMEM((len(pairs), 2 * rows * width, lanes), jnp.bfloat16)],
        compiler_params=PARAMS,
        name="partial_sums",
    )(numbers, *flat, *slip_groups)


BUFFERS = 4


def finish_kernel(first, width, has_sums, has_out, numbers_ref, rise_ref, *refs):
    pair = refs[:width]
    refs = refs[width:]
    slips_ref = refs[0]
    sums_ref = refs[1] if has_sums else None
    out_ref, table, buffers, sems = refs[-4:]
    count = slips_ref.shape[0]

    def copy(k):
        slot = k % BUFFERS
        return pltpu.make_async_copy(buffers.at[slot], out_ref.at[first + k], sems.at[slot])

    def body(k, carry):
        total = unit_sum(k, k, numbers_ref[1], pair, slips_ref, numbers_ref[0], table)
        if has_sums:
            total += sums_ref[k]
        stations = total.shape[0] // 2
        re, im = total[:stations], total[stations:]
        pulsation = (first + k + 1).astype(jnp.float32) * (2.0 * jnp.pi * BASE_FREQ)
        damping = pulsation * rise_ref[...]
        scale = 1.0 / (1.0 + damping * damping)
        tilt = scale * damping

        @pl.when(k >= BUFFERS)
        def _():
            copy(k - BUFFERS).wait()

        buffers[k % BUFFERS, 0] = scale * re + tilt * im
        buffers[k % BUFFERS, 1] = scale * im - tilt * re
        copy(k).start()
        return carry

    lax.fori_loop(0, count, body, 0)
    for k in range(max(0, count - BUFFERS), count):
        copy(k).wait()


def finish(first, total, numbers, rise_time, pair, slip_group, sums, so_far):
    rows, lanes = pair[0].shape[1:]
    stations = lanes // 2
    variations = slip_group.shape[2]
    args = [numbers, rise_time[None, :], *pair, slip_group]
    specs = [SMEM] + [VMEM] * (len(args) - 1)
    if sums is not None:
        args.append(sums)
        specs.append(VMEM)
    aliases = {}
    if so_far is not None:
        aliases = {len(args): 0}
        args.append(so_far)
        specs.append(ANY)
    return pl.pallas_call(
        functools.partial(finish_kernel, first, len(pair), sums is not None, so_far is not None),
        out_shape=jax.ShapeDtypeStruct((total, 2, stations, variations), jnp.float32),
        in_specs=specs,
        out_specs=ANY,
        scratch_shapes=[
            pltpu.VMEM((2 * rows * len(pair), lanes), jnp.bfloat16),
            pltpu.VMEM((BUFFERS, 2, stations, variations), jnp.float32),
            pltpu.SemaphoreType.DMA((BUFFERS,)),
        ],
        input_output_aliases=aliases,
        compiler_params=PARAMS,
        name="finish",
    )(*args)


def swap(array, axis):
    return lax.ppermute(array, axis, [(0, 1), (1, 0)])


def shards(size, fault_points, hypocenter, velocity, rise_time, member_mask, slip_amount, moment_tensor, strain_green, station_ids):
    freqs = strain_green.shape[4]
    half = moment_tensor.shape[1]
    own_part, other_part = rotate(strain_green[:, :, 0], moment_tensor, station_ids)
    received = swap(other_part, "sub")
    if size == 8:
        rows = own_part.shape[1]
        block = jnp.concatenate([own_part, received], axis=1)
        member_mask, slip_amount, block = lax.optimization_barrier((member_mask, slip_amount, block))
    else:
        rows = half
        whole = [lax.all_gather(piece, "var", axis=1, tiled=True) for piece in (own_part, received)]
        block = jnp.concatenate(whole, axis=1)
    own = amounts(member_mask, slip_amount)
    groups = (freqs // 2, freqs - freqs // 2)
    slip_groups = slips(groups, rows, fault_points, hypocenter, velocity, own, swap(own, "sub"))
    place = lax.axis_index("var")
    out = None
    first = 0
    if size != 8:
        numbers = jnp.zeros((2,), jnp.int32)
        for group in slip_groups:
            out = finish(first, freqs, numbers, rise_time, [block[first : first + group.shape[0]]], group, None, out)
            first += group.shape[0]
        return out
    along = lambda piece, s: lax.ppermute(piece, "var", [(i, (i + 2 * s) % 8) for i in range(8)])
    across = lambda piece: lax.ppermute(piece, "var", [(i, i ^ 1) for i in range(8)])
    parts = [along(block, 1), along(block, 3)]
    last = []
    for group in groups:
        last.append(along(block[first : first + group], 2))
        first += group
    flip = place % 2
    unit = lambda s: ((place - 2 * s) % 8) // 2
    numbers = jnp.stack([flip, unit(0), unit(1), unit(3)]).astype(jnp.int32)
    pairs = [(piece, across(piece)) for piece in [block] + parts]
    sums = partial_sums(numbers, pairs, slip_groups)
    numbers = jnp.stack([flip, unit(2)]).astype(jnp.int32)
    first = 0
    for piece, group, total in zip(last, slip_groups, sums):
        out = finish(first, freqs, numbers, rise_time, (piece, across(piece)), group, total, out)
        first += group.shape[0]
    return out


def solution(mesh):
    placed = (
        P(None, "site"),
        P(("site", "var")),
        P(("site", "var")),
        P(("site", "var")),
        P(("site", "var"), "sub"),
        P(("site", "var"), "sub"),
        P(None, ("site", "sub")),
        P("site", None, "sub", "var", None, None),
        P("site"),
    )
    return jax.shard_map(
        functools.partial(shards, mesh.shape["var"]),
        mesh=mesh,
        in_specs=placed,
        out_specs=P(None, None, "sub", ("site", "var")),
        check_vma=False,
    )
```

```python
import functools

import jax
import jax.numpy as jnp
from jax import lax
from jax.experimental import pallas as pl
from jax.experimental.pallas import tpu as pltpu
from jax.sharding import PartitionSpec as P

VMEM = pl.BlockSpec(memory_space=pltpu.VMEM)
SMEM = pl.BlockSpec(memory_space=pltpu.SMEM)
ANY = pl.BlockSpec(memory_space=pl.ANY)
ROOMY = pltpu.CompilerParams(vmem_limit_bytes=56 * 2**20)
SMALL = pltpu.CompilerParams(vmem_limit_bytes=12 * 2**20)
BASE_FREQ = 0.0625
LANES = 256
BLOCK = 128
UNITS = 4


def cost(microseconds):
    return pl.CostEstimate(flops=int(microseconds * 1.1e9), bytes_accessed=int(microseconds * 3e6), transcendentals=0)


def rotate_kernel(green_ref, tensor_ref, ids_ref, own_ref, other_ref, sums, rows):
    _, comps, count, freqs, stations = green_ref.shape
    half = stations // 2
    first = lax.axis_index("var") * count

    def one_subfault(m, carry):
        for part in range(2):
            total = green_ref[part, 0, m].astype(jnp.float32) * tensor_ref[0, first + m]
            for comp in range(1, comps):
                total = total + green_ref[part, comp, m].astype(jnp.float32) * tensor_ref[comp, first + m]
            at = pl.ds(pl.multiple_of(m * freqs, freqs), freqs)
            sums[at, part * stations : (part + 1) * stations] = total.astype(jnp.bfloat16)
        return carry

    lax.fori_loop(0, count, one_subfault, 0, unroll=4)

    lane = lax.broadcasted_iota(jnp.int32, (1, stations), 1)
    ids = ids_ref[...]
    turned = pltpu.roll(ids, half, 1)
    low = jnp.where(lane < half, ids, turned)
    high = jnp.where(lane < half, turned, ids)
    is_first = lax.axis_index("sub") == 0
    wanted = jnp.concatenate([jnp.where(is_first, low, high), jnp.where(is_first, high, low)], axis=1)
    row = lax.broadcasted_iota(jnp.int32, (2 * stations, 2 * stations), 0)
    column = lax.broadcasted_iota(jnp.int32, (2 * stations, 2 * stations), 1)
    part_of_column = (column // half) % 2
    picks = (row == wanted + part_of_column * stations).astype(jnp.float32).astype(jnp.bfloat16)
    picked = jnp.dot(sums[...], picks, preferred_element_type=jnp.float32)
    rows[0] = picked[:, :stations]
    rows[1] = picked[:, stations:]
    for k in range(freqs):
        at = pl.ds(k, count, stride=freqs)
        own_ref[k] = rows[0, at, :].astype(jnp.bfloat16)
        other_ref[k] = rows[1, at, :].astype(jnp.bfloat16)


def rotate(green, tensor, station_ids):
    _, _, count, freqs, stations = green.shape
    piece = jax.ShapeDtypeStruct((freqs, count, stations), jnp.bfloat16)
    return pl.pallas_call(
        rotate_kernel,
        out_shape=(piece, piece),
        in_specs=[VMEM, SMEM, VMEM],
        out_specs=(VMEM, VMEM),
        scratch_shapes=[
            pltpu.VMEM((count * freqs, 2 * stations), jnp.bfloat16),
            pltpu.VMEM((2, count * freqs, stations), jnp.float32),
        ],
        compiler_params=ROOMY,
        cost_estimate=cost(3),
        name="rotate",
    )(green, tensor, station_ids.reshape((1, stations)))


TOKEN = jax.ShapeDtypeStruct((8, 128), jnp.float32)


def prepare_kernel(
    points_ref, hypocenter_ref, velocity_ref, own_mask, own_slip, other_mask, other_slip, after_ref, *outs
):
    own_out, other_out, columns, spots, token = outs
    half, variations = own_out.shape
    subfaults = 2 * half
    token[...] = jnp.zeros_like(token)
    first = pl.multiple_of(lax.axis_index("sub") * half, half)
    second = pl.multiple_of(half - first, half)
    for axis in range(2):
        for at, start in ((0, first), (half, second)):
            wide = jnp.broadcast_to(points_ref[axis : axis + 1, pl.ds(start, half)], (BLOCK, half))
            columns[axis, at : at + half, :] = wide.T

    rest = points_ref[...]
    thirds = []
    for _ in range(3):
        thirds.append(rest.astype(jnp.bfloat16))
        rest = rest - thirds[-1].astype(jnp.float32)
    thirds = jnp.concatenate([t.astype(jnp.float32) for t in thirds], axis=0).astype(jnp.bfloat16)
    for lane in range(0, variations, LANES):
        lanes = slice(lane, lane + LANES)
        index = lax.broadcasted_iota(jnp.int32, (subfaults, LANES), 0)
        here = (index == hypocenter_ref[0:1, lanes]).astype(jnp.float32).astype(jnp.bfloat16)
        spot = jnp.dot(thirds, here, preferred_element_type=jnp.float32)
        spots[0:2, lanes] = (spot[0:2] + spot[2:4]) + spot[4:6]
        spots[2:3, lanes] = BASE_FREQ / velocity_ref[0:1, lanes]

    for mask, slip, out in ((own_mask, own_slip, own_out), (other_mask, other_slip, other_out)):
        for row in range(0, variations, BLOCK):
            rows = slice(row, row + BLOCK)
            out[:, rows] = (mask[rows, :].astype(jnp.float32) * slip[rows, :]).T


def prepare(points, hypocenter, velocity, own_mask, own_slip, other_mask, other_slip, after):
    variations, half = own_mask.shape
    out = jax.ShapeDtypeStruct((half, variations), jnp.float32)
    columns = jax.ShapeDtypeStruct((2, 2 * half, BLOCK), jnp.float32)
    spots = jax.ShapeDtypeStruct((8, variations), jnp.float32)
    return pl.pallas_call(
        prepare_kernel,
        out_shape=(out, out, columns, spots, TOKEN),
        in_specs=[VMEM] * 7 + [ANY],
        out_specs=(VMEM,) * 5,
        compiler_params=SMALL,
        cost_estimate=cost(3),
        name="prepare",
    )(points, hypocenter[None, :], velocity[None, :], own_mask, own_slip, other_mask, other_slip, after)


SIN = (3.14159264, -5.16771008, 2.55007751, -0.598291190, 0.0776574420)
COS = (0.999999953, -4.93479283, 4.05841131, -1.33187624, 0.219688854)


def sine_cosine(turns):
    rest = turns - jnp.floor(turns + 0.5)
    square = rest * rest
    sine = SIN[-1]
    for c in SIN[-2::-1]:
        sine = sine * square + c
    sine = sine * rest
    cosine = COS[-1]
    for c in COS[-2::-1]:
        cosine = cosine * square + c
    return 2.0 * sine * cosine, 1.0 - 2.0 * sine * sine


def fill(slips_ref, numbers_ref, unit, step, columns, spots, own_ref, other_ref):
    freqs, _, depth, _ = slips_ref.shape
    half = own_ref.shape[0]
    rows = depth // 8
    piece, block = step % 2, step // 2
    row = pl.multiple_of((2 * numbers_ref[1 + unit] + (piece ^ numbers_ref[0])) * rows, rows)
    lanes = pl.ds(pl.multiple_of(block * BLOCK, BLOCK), BLOCK)
    for part, source in enumerate((own_ref, other_ref)):
        at = pl.ds(part * half + row, rows)
        east = columns[0, at, :] - spots[0:1, lanes]
        north = columns[1, at, :] - spots[1:2, lanes]
        gap = east * east + north * north
        distance = gap * lax.rsqrt(jnp.maximum(gap, 1e-30))
        sine, cosine = sine_cosine(distance * spots[2:3, lanes])
        amount = source[pl.ds(row, rows), lanes]
        twice = 2.0 * cosine
        re_last, im_last = amount, None
        re, im = amount * cosine, amount * sine
        place = pl.multiple_of((4 * piece + part) * rows, rows)
        for k in range(freqs):
            slips_ref[k, block, pl.ds(place, rows), :] = re.astype(jnp.bfloat16)
            slips_ref[k, block, pl.ds(place + 2 * rows, rows), :] = im.astype(jnp.bfloat16)
            re, re_last = twice * re - re_last, re
            im, im_last = (twice * im if im_last is None else twice * im - im_last), im


def unit_sum(k, first, pair, slips_ref):
    half = pair[0].shape[2] // 2
    lane = lax.broadcasted_iota(jnp.int32, (1, 2 * half), 1)
    table = []
    for ref in pair:
        block = ref[k]
        turned = pltpu.roll(block.astype(jnp.float32), half, 1)
        table += [block, jnp.where(lane < half, turned, -turned).astype(jnp.bfloat16)]
    wide = jnp.concatenate([slips_ref[first + k, block] for block in range(slips_ref.shape[1])], axis=1)
    return lax.dot_general(
        jnp.concatenate(table, axis=0), wide, (((0,), (0,)), ((), ())), preferred_element_type=jnp.float32
    )


def work_kernel(fills, has_sum, has_total, unroll, numbers_ref, *refs):
    refs = list(refs)
    take = lambda n: [refs.pop(0) for _ in range(n)]
    sources = take(4) if fills else None
    pair, (slips_ref,) = (take(2), take(1)) if has_sum else (None, (None,))
    (total_ref,) = take(1) if has_total else (None,)
    token = refs.pop()
    (sum_ref,) = [refs.pop()] if has_sum else (None,)
    outs = refs[len(refs) - len(fills) :]
    token[...] = jnp.zeros_like(token)

    def body(k, carry):
        for unit, out in zip(fills, outs):
            fill(out, numbers_ref, unit, k, *sources)
        if has_sum:
            term = unit_sum(k, 0, pair, slips_ref)
            sum_ref[k] = term + total_ref[k] if has_total else term
        return carry

    lax.fori_loop(0, FREQS, body, 0, unroll=unroll)


FREQS = 16


def work(numbers, sources, fills, pair=None, unit_slips=None, total=None, after=()):
    columns, spots, own, other = sources
    variations = own.shape[1]
    freqs = FREQS
    args, aliases = [numbers], {}
    if fills:
        args += sources
    shapes = [
        jax.ShapeDtypeStruct((freqs, variations // BLOCK, 4 * own.shape[0] // UNITS, BLOCK), jnp.bfloat16)
    ] * len(fills)
    if pair is not None:
        args += [*pair, unit_slips]
        if total is not None:
            aliases = {len(args): len(shapes)}
            args.append(total)
        shapes.append(jax.ShapeDtypeStruct((freqs, pair[0].shape[2], variations), jnp.float32))
    shapes.append(TOKEN)
    return pl.pallas_call(
        functools.partial(work_kernel, fills, pair is not None, total is not None, 1 if len(fills) > 1 else 2),
        out_shape=tuple(shapes),
        in_specs=[SMEM] + [VMEM] * (len(args) - 1) + [ANY] * len(after),
        out_specs=(VMEM,) * len(shapes),
        input_output_aliases=aliases,
        compiler_params=SMALL,
        cost_estimate=cost(3),
        name="work" + "".join(str(u) for u in fills) + ("_sum" if pair is not None else ""),
    )(*args, *after)


def finish_kernel(first, count, rise_ref, *refs):
    pair, slips_ref, sums_ref = refs[:2], refs[2], refs[3]
    out_ref, buffers, sems = refs[-3:]

    def copy(k):
        return pltpu.make_async_copy(buffers.at[k], out_ref.at[first + k], sems.at[k])

    def body(k, carry):
        total = sums_ref[first + k] + unit_sum(k, first, pair, slips_ref)
        stations = total.shape[0] // 2
        re, im = total[:stations], total[stations:]
        pulsation = (first + k + 1).astype(jnp.float32) * (2.0 * jnp.pi * BASE_FREQ)
        damping = pulsation * rise_ref[...]
        scale = 1.0 / (1.0 + damping * damping)
        tilt = scale * damping
        buffers[k, 0] = scale * re + tilt * im
        buffers[k, 1] = scale * im - tilt * re
        copy(k).start()
        return carry

    lax.fori_loop(0, count, body, 0, unroll=2)
    for k in range(count):
        copy(k).wait()


def finish(first, rise_time, pair, unit_slips, sums, so_far):
    count, _, lanes = pair[0].shape
    stations = lanes // 2
    total, _, variations = sums.shape
    args = [rise_time[None, :], *pair, unit_slips, sums]
    specs = [VMEM] * len(args)
    aliases = {}
    if so_far is not None:
        aliases = {len(args): 0}
        args.append(so_far)
        specs.append(ANY)
    return pl.pallas_call(
        functools.partial(finish_kernel, first, count),
        out_shape=jax.ShapeDtypeStruct((total, 2, stations, variations), jnp.float32),
        in_specs=specs,
        out_specs=ANY,
        scratch_shapes=[
            pltpu.VMEM((count, 2, stations, variations), jnp.float32),
            pltpu.SemaphoreType.DMA((count,)),
        ],
        input_output_aliases=aliases,
        compiler_params=SMALL,
        cost_estimate=cost(2),
        name="finish",
    )(*args)


def swap(array, axis):
    return lax.ppermute(array, axis, [(0, 1), (1, 0)])


def along(piece, s):
    return lax.ppermute(piece, "var", [(i, (i + 2 * s) % 8) for i in range(8)])


def across(piece):
    return lax.ppermute(piece, "var", [(i, i ^ 1) for i in range(8)])


def gate_kernel(array_ref, token_ref, out_ref):
    pass


def gate(array, token):
    return pl.pallas_call(
        gate_kernel,
        out_shape=jax.ShapeDtypeStruct(array.shape, array.dtype),
        in_specs=[ANY, ANY],
        out_specs=ANY,
        input_output_aliases={0: 0},
        compiler_params=SMALL,
        name="gate",
    )(array, token)


def shards(size, fault_points, hypocenter, velocity, rise_time, member_mask, slip_amount, moment_tensor, strain_green, station_ids):
    freqs = strain_green.shape[4]
    half = moment_tensor.shape[1]
    rows = half // (2 * UNITS)
    groups = (freqs // 2, freqs - freqs // 2)
    cuts = ((0, groups[0]), (groups[0], freqs))
    swapped = [swap(array, "sub") for array in (member_mask, slip_amount)]
    own_part, other_part = rotate(strain_green[:, :, 0], moment_tensor, station_ids)
    received = swap(other_part, "sub")
    routed = size == 2 * UNITS
    if routed:
        place = lax.axis_index("var")
        block = jnp.concatenate([own_part, received], axis=1)
        pieces = [block, along(block, 1), along(block, 3)]
        numbers = jnp.stack([place % 2] + [((place - 2 * s) % 8) // 2 for s in (0, 1, 3, 2)]).astype(jnp.int32)
    else:
        whole = [lax.all_gather(piece, "var", axis=1, tiled=True) for piece in (own_part, received)]
        pieces = [
            jnp.concatenate([part[:, i * rows : (i + 1) * rows] for part in whole], axis=1) for i in range(2 * UNITS)
        ]
        pairs = [(pieces[2 * i], pieces[2 * i + 1]) for i in range(UNITS)]
        last = [tuple(piece[i:j] for piece in pairs[-1]) for i, j in cuts]
        numbers = jnp.arange(-1, UNITS, dtype=jnp.int32) * (jnp.arange(1 + UNITS, dtype=jnp.int32) > 0)

    own, other, columns, spots, token = prepare(
        fault_points, hypocenter, velocity, member_mask, slip_amount, *swapped, pieces[0]
    )
    step = functools.partial(work, numbers, (columns, spots, own, other))
    if routed:
        parts = [gate(block[i:j], token) for i, j in cuts]
        last = [along(part, 2) for part in parts]
        pairs = [(block, across(block))]
    else:
        parts = (token,)
    slips_0, slips_1, token = step((0, 1), after=parts)
    if routed:
        pieces[1] = gate(pieces[1], token)
        pairs.append((pieces[1], across(pieces[1])))
    slips_3, total, token = step((2,), pairs[0], slips_0, after=pieces[1:2])
    if routed:
        pieces[2] = gate(pieces[2], token)
        pairs.append((pieces[2], across(pieces[2])))
    slips_2, total, token = step((3,), pairs[1], slips_1, total, after=pieces[2:3])
    if routed:
        last = [gate(piece, token) for piece in last]
        last = [(piece, across(piece)) for piece in last]
    total, token = step((), pairs[2], slips_3, total, after=(last[0][0], last[1][0]))
    out = None
    for (first, _), pair in zip(cuts, last):
        out = finish(first, rise_time, pair, slips_2, total, out)
    return out


def solution(mesh):
    placed = (
        P(None, "site"),
        P(("site", "var")),
        P(("site", "var")),
        P(("site", "var")),
        P(("site", "var"), "sub"),
        P(("site", "var"), "sub"),
        P(None, ("site", "sub")),
        P("site", None, "sub", "var", None, None),
        P("site"),
    )
    return jax.shard_map(
        functools.partial(shards, mesh.shape["var"]),
        mesh=mesh,
        in_specs=placed,
        out_specs=P(None, None, "sub", ("site", "var")),
        check_vma=False,
    )
```

```python
import functools

import jax
import jax.numpy as jnp
from jax import lax
from jax.experimental import pallas as pl
from jax.experimental.pallas import tpu as pltpu
from jax.sharding import PartitionSpec as P

VMEM = pl.BlockSpec(memory_space=pltpu.VMEM)
SMEM = pl.BlockSpec(memory_space=pltpu.SMEM)
ANY = pl.BlockSpec(memory_space=pl.ANY)
ROOMY = pltpu.CompilerParams(vmem_limit_bytes=56 * 2**20)
SMALL = pltpu.CompilerParams(vmem_limit_bytes=12 * 2**20)
BASE_FREQ = 0.0625
LANES = 256
BLOCK = 128
UNITS = 4


def cost(microseconds):
    return pl.CostEstimate(flops=int(microseconds * 1.1e9), bytes_accessed=int(microseconds * 3e6), transcendentals=0)


def rotate_kernel(green_ref, tensor_ref, ids_ref, own_ref, other_ref, sums, rows):
    _, comps, count, freqs, stations = green_ref.shape
    half = stations // 2
    first = lax.axis_index("var") * count

    def one_subfault(m, carry):
        for part in range(2):
            total = green_ref[part, 0, m].astype(jnp.float32) * tensor_ref[0, first + m]
            for comp in range(1, comps):
                total = total + green_ref[part, comp, m].astype(jnp.float32) * tensor_ref[comp, first + m]
            at = pl.ds(pl.multiple_of(m * freqs, freqs), freqs)
            sums[at, part * stations : (part + 1) * stations] = total.astype(jnp.bfloat16)
        return carry

    lax.fori_loop(0, count, one_subfault, 0, unroll=4)

    lane = lax.broadcasted_iota(jnp.int32, (1, stations), 1)
    ids = ids_ref[...]
    turned = pltpu.roll(ids, half, 1)
    low = jnp.where(lane < half, ids, turned)
    high = jnp.where(lane < half, turned, ids)
    is_first = lax.axis_index("sub") == 0
    wanted = jnp.concatenate([jnp.where(is_first, low, high), jnp.where(is_first, high, low)], axis=1)
    row = lax.broadcasted_iota(jnp.int32, (2 * stations, 2 * stations), 0)
    column = lax.broadcasted_iota(jnp.int32, (2 * stations, 2 * stations), 1)
    part_of_column = (column // half) % 2
    picks = (row == wanted + part_of_column * stations).astype(jnp.float32).astype(jnp.bfloat16)
    picked = jnp.dot(sums[...], picks, preferred_element_type=jnp.float32)
    rows[0] = picked[:, :stations]
    rows[1] = picked[:, stations:]
    for k in range(freqs):
        at = pl.ds(k, count, stride=freqs)
        own_ref[k] = rows[0, at, :].astype(jnp.bfloat16)
        other_ref[k] = rows[1, at, :].astype(jnp.bfloat16)


def rotate(green, tensor, station_ids):
    _, _, count, freqs, stations = green.shape
    piece = jax.ShapeDtypeStruct((freqs, count, stations), jnp.bfloat16)
    return pl.pallas_call(
        rotate_kernel,
        out_shape=(piece, piece),
        in_specs=[VMEM, SMEM, VMEM],
        out_specs=(VMEM, VMEM),
        scratch_shapes=[
            pltpu.VMEM((count * freqs, 2 * stations), jnp.bfloat16),
            pltpu.VMEM((2, count * freqs, stations), jnp.float32),
        ],
        compiler_params=ROOMY,
        cost_estimate=cost(3),
        name="rotate",
    )(green, tensor, station_ids.reshape((1, stations)))


TOKEN = jax.ShapeDtypeStruct((8, 128), jnp.float32)


def prepare_kernel(
    points_ref, hypocenter_ref, velocity_ref, own_mask, own_slip, other_mask, other_slip, after_ref, *outs
):
    own_out, other_out, columns, spots, token = outs
    half, variations = own_out.shape
    subfaults = 2 * half
    token[...] = jnp.zeros_like(token)
    first = pl.multiple_of(lax.axis_index("sub") * half, half)
    second = pl.multiple_of(half - first, half)
    for axis in range(2):
        for at, start in ((0, first), (half, second)):
            wide = jnp.broadcast_to(points_ref[axis : axis + 1, pl.ds(start, half)], (BLOCK, half))
            columns[axis, at : at + half, :] = wide.T

    rest = points_ref[...]
    thirds = []
    for _ in range(3):
        thirds.append(rest.astype(jnp.bfloat16))
        rest = rest - thirds[-1].astype(jnp.float32)
    thirds = jnp.concatenate([t.astype(jnp.float32) for t in thirds], axis=0).astype(jnp.bfloat16)
    for lane in range(0, variations, LANES):
        lanes = slice(lane, lane + LANES)
        index = lax.broadcasted_iota(jnp.int32, (subfaults, LANES), 0)
        here = (index == hypocenter_ref[0:1, lanes]).astype(jnp.float32).astype(jnp.bfloat16)
        spot = jnp.dot(thirds, here, preferred_element_type=jnp.float32)
        spots[0:2, lanes] = (spot[0:2] + spot[2:4]) + spot[4:6]
        spots[2:3, lanes] = BASE_FREQ / velocity_ref[0:1, lanes]

    for mask, slip, out in ((own_mask, own_slip, own_out), (other_mask, other_slip, other_out)):
        for row in range(0, variations, BLOCK):
            rows = slice(row, row + BLOCK)
            out[:, rows] = (mask[rows, :].astype(jnp.float32) * slip[rows, :]).T


def prepare(points, hypocenter, velocity, own_mask, own_slip, other_mask, other_slip, after):
    variations, half = own_mask.shape
    out = jax.ShapeDtypeStruct((half, variations), jnp.float32)
    columns = jax.ShapeDtypeStruct((2, 2 * half, BLOCK), jnp.float32)
    spots = jax.ShapeDtypeStruct((8, variations), jnp.float32)
    return pl.pallas_call(
        prepare_kernel,
        out_shape=(out, out, columns, spots, TOKEN),
        in_specs=[VMEM] * 7 + [ANY],
        out_specs=(VMEM,) * 5,
        compiler_params=SMALL,
        cost_estimate=cost(3),
        name="prepare",
    )(points, hypocenter[None, :], velocity[None, :], own_mask, own_slip, other_mask, other_slip, after)


SIN = (3.14159264, -5.16771008, 2.55007751, -0.598291190, 0.0776574420)
COS = (0.999999953, -4.93479283, 4.05841131, -1.33187624, 0.219688854)


def sine_cosine(turns):
    rest = turns - jnp.floor(turns + 0.5)
    square = rest * rest
    sine = SIN[-1]
    for c in SIN[-2::-1]:
        sine = sine * square + c
    sine = sine * rest
    cosine = COS[-1]
    for c in COS[-2::-1]:
        cosine = cosine * square + c
    return 2.0 * sine * cosine, 1.0 - 2.0 * sine * sine


def fill(slips_ref, numbers_ref, unit, step, columns, spots, own_ref, other_ref):
    freqs, _, depth, _ = slips_ref.shape
    half = own_ref.shape[0]
    rows = depth // 8
    piece, block = step % 2, step // 2
    row = pl.multiple_of((2 * numbers_ref[1 + unit] + (piece ^ numbers_ref[0])) * rows, rows)
    lanes = pl.ds(pl.multiple_of(block * BLOCK, BLOCK), BLOCK)
    for part, source in enumerate((own_ref, other_ref)):
        at = pl.ds(part * half + row, rows)
        east = columns[0, at, :] - spots[0:1, lanes]
        north = columns[1, at, :] - spots[1:2, lanes]
        gap = east * east + north * north
        distance = gap * lax.rsqrt(jnp.maximum(gap, 1e-30))
        sine, cosine = sine_cosine(distance * spots[2:3, lanes])
        amount = source[pl.ds(row, rows), lanes]
        twice = 2.0 * cosine
        re_last, im_last = amount, None
        re, im = amount * cosine, amount * sine
        place = pl.multiple_of((4 * piece + part) * rows, rows)
        for k in range(freqs):
            slips_ref[k, block, pl.ds(place, rows), :] = re.astype(jnp.bfloat16)
            slips_ref[k, block, pl.ds(place + 2 * rows, rows), :] = im.astype(jnp.bfloat16)
            re, re_last = twice * re - re_last, re
            im, im_last = (twice * im if im_last is None else twice * im - im_last), im


def sum_of(k, first, pairs, slip_refs):
    half = pairs[0][0].shape[2] // 2
    lane = lax.broadcasted_iota(jnp.int32, (1, 2 * half), 1)
    table, wide = [], []
    for pair, slips_ref in zip(pairs, slip_refs):
        for ref in pair:
            block = ref[k]
            turned = pltpu.roll(block.astype(jnp.float32), half, 1)
            table += [block, jnp.where(lane < half, turned, -turned).astype(jnp.bfloat16)]
        wide.append(jnp.concatenate([slips_ref[first + k, block] for block in range(slips_ref.shape[1])], axis=1))
    return lax.dot_general(
        jnp.concatenate(table, axis=0),
        jnp.concatenate(wide, axis=0),
        (((0,), (0,)), ((), ())),
        preferred_element_type=jnp.float32,
    )


def work_kernel(fills, sums, has_total, unroll, numbers_ref, *refs):
    refs = list(refs)
    take = lambda n: [refs.pop(0) for _ in range(n)]
    sources = take(4) if fills else None
    pairs, slip_refs = [], []
    for _ in range(sums):
        pairs.append(take(2))
        slip_refs += take(1)
    total_ref = take(1)[0] if has_total else None
    token = refs.pop()
    sum_ref = refs.pop() if sums else None
    outs = refs[len(refs) - len(fills) :]
    token[...] = jnp.zeros_like(token)

    def body(k, carry):
        if sums:
            term = sum_of(k, 0, pairs, slip_refs)
            sum_ref[k] = term + total_ref[k] if has_total else term
        for unit, out in zip(fills, outs):
            fill(out, numbers_ref, unit, k, *sources)
        return carry

    lax.fori_loop(0, FREQS, body, 0, unroll=unroll)


FREQS = 16


def work(numbers, sources, fills, sums=(), total=None, after=(), unroll=2):
    columns, spots, own, other = sources
    variations = own.shape[1]
    args, aliases = [numbers], {}
    if fills:
        args += sources
    shapes = [
        jax.ShapeDtypeStruct((FREQS, variations // BLOCK, 4 * own.shape[0] // UNITS, BLOCK), jnp.bfloat16)
    ] * len(fills)
    for pair, unit_slips in sums:
        args += [*pair, unit_slips]
    if sums:
        if total is not None:
            aliases = {len(args): len(shapes)}
            args.append(total)
        shapes.append(jax.ShapeDtypeStruct((FREQS, sums[0][0][0].shape[2], variations), jnp.float32))
    shapes.append(TOKEN)
    return pl.pallas_call(
        functools.partial(work_kernel, fills, len(sums), total is not None, unroll),
        out_shape=tuple(shapes),
        in_specs=[SMEM] + [VMEM] * (len(args) - 1) + [ANY] * len(after),
        out_specs=(VMEM,) * len(shapes),
        input_output_aliases=aliases,
        compiler_params=SMALL,
        cost_estimate=cost(3),
        name="fill" * len(fills) + "sum" * len(sums),
    )(*args, *after)


def finish_kernel(first, count, rise_ref, *refs):
    pair, slips_ref, sums_ref = refs[:2], refs[2], refs[3]
    out_ref, buffers, sems = refs[-3:]

    def copy(k):
        return pltpu.make_async_copy(buffers.at[k], out_ref.at[first + k], sems.at[k])

    def body(k, carry):
        total = sums_ref[first + k] + sum_of(k, first, [pair], [slips_ref])
        stations = total.shape[0] // 2
        re, im = total[:stations], total[stations:]
        pulsation = (first + k + 1).astype(jnp.float32) * (2.0 * jnp.pi * BASE_FREQ)
        damping = pulsation * rise_ref[...]
        scale = 1.0 / (1.0 + damping * damping)
        tilt = scale * damping
        buffers[k, 0] = scale * re + tilt * im
        buffers[k, 1] = scale * im - tilt * re
        copy(k).start()
        return carry

    lax.fori_loop(0, count, body, 0, unroll=4)
    for k in range(count):
        copy(k).wait()


def finish(first, rise_time, pair, unit_slips, sums, so_far):
    count, _, lanes = pair[0].shape
    stations = lanes // 2
    total, _, variations = sums.shape
    args = [rise_time[None, :], *pair, unit_slips, sums]
    specs = [VMEM] * len(args)
    aliases = {}
    if so_far is not None:
        aliases = {len(args): 0}
        args.append(so_far)
        specs.append(ANY)
    return pl.pallas_call(
        functools.partial(finish_kernel, first, count),
        out_shape=jax.ShapeDtypeStruct((total, 2, stations, variations), jnp.float32),
        in_specs=specs,
        out_specs=ANY,
        scratch_shapes=[
            pltpu.VMEM((count, 2, stations, variations), jnp.float32),
            pltpu.SemaphoreType.DMA((count,)),
        ],
        input_output_aliases=aliases,
        compiler_params=SMALL,
        cost_estimate=cost(2),
        name="finish",
    )(*args)


def swap(array, axis):
    return lax.ppermute(array, axis, [(0, 1), (1, 0)])


def along(piece, s):
    return lax.ppermute(piece, "var", [(i, i ^ (2 * s)) for i in range(8)])


def across(piece):
    return lax.ppermute(piece, "var", [(i, i ^ 1) for i in range(8)])


def gate_kernel(array_ref, token_ref, out_ref):
    pass


def gate(array, token):
    return pl.pallas_call(
        gate_kernel,
        out_shape=jax.ShapeDtypeStruct(array.shape, array.dtype),
        in_specs=[ANY, ANY],
        out_specs=ANY,
        input_output_aliases={0: 0},
        compiler_params=SMALL,
        name="gate",
    )(array, token)


def shards(size, fault_points, hypocenter, velocity, rise_time, member_mask, slip_amount, moment_tensor, strain_green, station_ids):
    freqs = strain_green.shape[4]
    half = moment_tensor.shape[1]
    rows = half // (2 * UNITS)
    groups = (freqs // 2, freqs - freqs // 2)
    cuts = ((0, groups[0]), (groups[0], freqs))
    swapped = [swap(array, "sub") for array in (member_mask, slip_amount)]
    own_part, other_part = rotate(strain_green[:, :, 0], moment_tensor, station_ids)
    received = swap(other_part, "sub")
    routed = size == 2 * UNITS
    if routed:
        place = lax.axis_index("var")
        block = jnp.concatenate([own_part, received], axis=1)
        pieces = [block, along(block, 1), along(block, 3)]
        numbers = jnp.stack([place % 2] + [(place // 2) ^ s for s in (0, 1, 3, 2)]).astype(jnp.int32)
    else:
        whole = [lax.all_gather(piece, "var", axis=1, tiled=True) for piece in (own_part, received)]
        pieces = [
            jnp.concatenate([part[:, i * rows : (i + 1) * rows] for part in whole], axis=1) for i in range(2 * UNITS)
        ]
        pairs = [(pieces[2 * i], pieces[2 * i + 1]) for i in range(UNITS)]
        last = [tuple(piece[i:j] for piece in pairs[-1]) for i, j in cuts]
        numbers = jnp.arange(-1, UNITS, dtype=jnp.int32) * (jnp.arange(1 + UNITS, dtype=jnp.int32) > 0)

    own, other, columns, spots, token = prepare(
        fault_points, hypocenter, velocity, member_mask, slip_amount, *swapped, pieces[0]
    )
    step = functools.partial(work, numbers, (columns, spots, own, other))
    slips_0, token = step((0,), after=(token,))
    if routed:
        last = [along(gate(block[i:j], token), 2) for i, j in cuts]
        pieces[1] = gate(pieces[1], token)
        pairs = [(piece, across(piece)) for piece in pieces[:2]]
    slips_1, slips_2, token = step((1, 2), after=pieces[1:2])
    if routed:
        pieces[2] = gate(pieces[2], token)
        pairs.append((pieces[2], across(pieces[2])))
    slips_3, total, token = step((3,), ((pairs[0], slips_0), (pairs[1], slips_1)), after=pieces[2:3], unroll=8)
    if routed:
        last = [gate(piece, token) for piece in last]
        last = [(piece, across(piece)) for piece in last]
    total, token = step((), ((pairs[2], slips_2),), total, after=(last[0][0], last[1][0]), unroll=8)
    out = None
    for (first, _), pair in zip(cuts, last):
        out = finish(first, rise_time, pair, slips_3, total, out)
    return out


def solution(mesh):
    placed = (
        P(None, "site"),
        P(("site", "var")),
        P(("site", "var")),
        P(("site", "var")),
        P(("site", "var"), "sub"),
        P(("site", "var"), "sub"),
        P(None, ("site", "sub")),
        P("site", None, "sub", "var", None, None),
        P("site"),
    )
    return jax.shard_map(
        functools.partial(shards, mesh.shape["var"]),
        mesh=mesh,
        in_specs=placed,
        out_specs=P(None, None, "sub", ("site", "var")),
        check_vma=False,
    )
```

```python
import functools

import jax
import jax.numpy as jnp
from jax import lax
from jax.experimental import pallas as pl
from jax.experimental.pallas import tpu as pltpu
from jax.sharding import PartitionSpec as P

VMEM = pl.BlockSpec(memory_space=pltpu.VMEM)
SMEM = pl.BlockSpec(memory_space=pltpu.SMEM)
ANY = pl.BlockSpec(memory_space=pl.ANY)
ROOMY = pltpu.CompilerParams(vmem_limit_bytes=56 * 2**20)
SMALL = pltpu.CompilerParams(vmem_limit_bytes=12 * 2**20)
BASE_FREQ = 0.0625
LANES = 256
BLOCK = 128
UNITS = 4


def cost(microseconds):
    return pl.CostEstimate(flops=int(microseconds * 1.1e9), bytes_accessed=int(microseconds * 3e6), transcendentals=0)


def rotate_kernel(green_hbm, tensor_hbm, ids_hbm, own_ref, other_ref, green, tensor_ref, ids_ref, sums, rows, sems, few):
    _, comps, count, freqs, stations = green.shape
    half = stations // 2
    first = lax.axis_index("var") * count

    def load(part, comp):
        return pltpu.make_async_copy(green_hbm.at[part, comp], green.at[part, comp], sems.at[part, comp])

    small = [
        pltpu.make_async_copy(ids_hbm, ids_ref, few.at[0]),
        pltpu.make_async_copy(tensor_hbm, tensor_ref, few.at[1]),
    ]
    for copy in small:
        copy.start()
    for part in range(2):
        for comp in range(comps):
            load(part, comp).start()
    for copy in small:
        copy.wait()

    lane = lax.broadcasted_iota(jnp.int32, (1, stations), 1)
    ids = ids_ref[...]
    turned = pltpu.roll(ids, half, 1)
    low = jnp.where(lane < half, ids, turned)
    high = jnp.where(lane < half, turned, ids)
    is_first = lax.axis_index("sub") == 0
    wanted = jnp.concatenate([jnp.where(is_first, low, high), jnp.where(is_first, high, low)], axis=1)
    row = lax.broadcasted_iota(jnp.int32, (2 * stations, 2 * stations), 0)
    column = lax.broadcasted_iota(jnp.int32, (2 * stations, 2 * stations), 1)
    part_of_column = (column // half) % 2
    picks = (row == wanted + part_of_column * stations).astype(jnp.float32).astype(jnp.bfloat16)

    for part in range(2):
        for comp in range(comps):
            load(part, comp).wait()

        def one_subfault(m, carry, part=part):
            total = green[part, 0, m].astype(jnp.float32) * tensor_ref[0, first + m]
            for comp in range(1, comps):
                total = total + green[part, comp, m].astype(jnp.float32) * tensor_ref[comp, first + m]
            at = pl.ds(pl.multiple_of(m * freqs, freqs), freqs)
            sums[at, part * stations : (part + 1) * stations] = total.astype(jnp.bfloat16)
            return carry

        lax.fori_loop(0, count, one_subfault, 0, unroll=8)
    picked = jnp.dot(sums[...], picks, preferred_element_type=jnp.float32)
    rows[0] = picked[:, :stations]
    rows[1] = picked[:, stations:]
    for k in range(freqs):
        at = pl.ds(k, count, stride=freqs)
        own_ref[k] = rows[0, at, :].astype(jnp.bfloat16)
        other_ref[k] = rows[1, at, :].astype(jnp.bfloat16)


def rotate(green, tensor, station_ids):
    _, _, count, freqs, stations = green.shape
    piece = jax.ShapeDtypeStruct((freqs, count, stations), jnp.bfloat16)
    return pl.pallas_call(
        rotate_kernel,
        out_shape=(piece, piece),
        in_specs=[ANY] * 3,
        out_specs=(VMEM, VMEM),
        scratch_shapes=[
            pltpu.VMEM(green.shape, jnp.bfloat16),
            pltpu.SMEM(tensor.shape, jnp.float32),
            pltpu.VMEM((1, stations), jnp.int32),
            pltpu.VMEM((count * freqs, 2 * stations), jnp.bfloat16),
            pltpu.VMEM((2, count * freqs, stations), jnp.float32),
            pltpu.SemaphoreType.DMA(green.shape[:2]),
            pltpu.SemaphoreType.DMA((2,)),
        ],
        compiler_params=ROOMY,
        cost_estimate=cost(3),
        name="rotate",
    )(green, tensor, station_ids.reshape((1, stations)))


TOKEN = jax.ShapeDtypeStruct((8, 128), jnp.float32)


def prepare_kernel(
    points_ref, hypocenter_ref, velocity_ref, own_mask, own_slip, other_mask, other_slip, after_ref, *outs
):
    own_out, other_out, columns, spots, token = outs
    half, variations = own_out.shape
    subfaults = 2 * half
    token[...] = jnp.zeros_like(token)
    first = pl.multiple_of(lax.axis_index("sub") * half, half)
    second = pl.multiple_of(half - first, half)
    for axis in range(2):
        for at, start in ((0, first), (half, second)):
            wide = jnp.broadcast_to(points_ref[axis : axis + 1, pl.ds(start, half)], (BLOCK, half))
            columns[axis, at : at + half, :] = wide.T

    rest = points_ref[...]
    thirds = []
    for _ in range(3):
        thirds.append(rest.astype(jnp.bfloat16))
        rest = rest - thirds[-1].astype(jnp.float32)
    thirds = jnp.concatenate([t.astype(jnp.float32) for t in thirds], axis=0).astype(jnp.bfloat16)
    for lane in range(0, variations, LANES):
        lanes = slice(lane, lane + LANES)
        index = lax.broadcasted_iota(jnp.int32, (subfaults, LANES), 0)
        here = (index == hypocenter_ref[0:1, lanes]).astype(jnp.float32).astype(jnp.bfloat16)
        spot = jnp.dot(thirds, here, preferred_element_type=jnp.float32)
        spots[0:2, lanes] = (spot[0:2] + spot[2:4]) + spot[4:6]
        spots[2:3, lanes] = BASE_FREQ / velocity_ref[0:1, lanes]

    for mask, slip, out in ((own_mask, own_slip, own_out), (other_mask, other_slip, other_out)):
        for row in range(0, variations, BLOCK):
            rows = slice(row, row + BLOCK)
            out[:, rows] = (mask[rows, :].astype(jnp.float32) * slip[rows, :]).T


def prepare(points, hypocenter, velocity, own_mask, own_slip, other_mask, other_slip, after):
    variations, half = own_mask.shape
    out = jax.ShapeDtypeStruct((half, variations), jnp.float32)
    columns = jax.ShapeDtypeStruct((2, 2 * half, BLOCK), jnp.float32)
    spots = jax.ShapeDtypeStruct((8, variations), jnp.float32)
    return pl.pallas_call(
        prepare_kernel,
        out_shape=(out, out, columns, spots, TOKEN),
        in_specs=[VMEM] * 7 + [ANY],
        out_specs=(VMEM,) * 5,
        compiler_params=SMALL,
        cost_estimate=cost(3),
        name="prepare",
    )(points, hypocenter[None, :], velocity[None, :], own_mask, own_slip, other_mask, other_slip, after)


SIN = (3.14159264, -5.16771008, 2.55007751, -0.598291190, 0.0776574420)
COS = (0.999999953, -4.93479283, 4.05841131, -1.33187624, 0.219688854)


def sine_cosine(turns):
    rest = turns - jnp.floor(turns + 0.5)
    square = rest * rest
    sine = SIN[-1]
    for c in SIN[-2::-1]:
        sine = sine * square + c
    sine = sine * rest
    cosine = COS[-1]
    for c in COS[-2::-1]:
        cosine = cosine * square + c
    return 2.0 * sine * cosine, 1.0 - 2.0 * sine * sine


def fill(slips_ref, numbers_ref, unit, step, columns, spots, own_ref, other_ref):
    freqs, _, depth, _ = slips_ref.shape
    half = own_ref.shape[0]
    rows = depth // 8
    piece, block = step % 2, step // 2
    row = pl.multiple_of((2 * numbers_ref[1 + unit] + (piece ^ numbers_ref[0])) * rows, rows)
    lanes = pl.ds(pl.multiple_of(block * BLOCK, BLOCK), BLOCK)
    for part, source in enumerate((own_ref, other_ref)):
        at = pl.ds(part * half + row, rows)
        east = columns[0, at, :] - spots[0:1, lanes]
        north = columns[1, at, :] - spots[1:2, lanes]
        gap = east * east + north * north
        distance = gap * lax.rsqrt(jnp.maximum(gap, 1e-30))
        sine, cosine = sine_cosine(distance * spots[2:3, lanes])
        amount = source[pl.ds(row, rows), lanes]
        twice = 2.0 * cosine
        re_last, im_last = amount, None
        re, im = amount * cosine, amount * sine
        place = pl.multiple_of((4 * piece + part) * rows, rows)
        for k in range(freqs):
            slips_ref[k, block, pl.ds(place, rows), :] = re.astype(jnp.bfloat16)
            slips_ref[k, block, pl.ds(place + 2 * rows, rows), :] = im.astype(jnp.bfloat16)
            re, re_last = twice * re - re_last, re
            im, im_last = (twice * im if im_last is None else twice * im - im_last), im


def sum_of(k, pairs, slip_refs):
    half = pairs[0][0].shape[2] // 2
    lane = lax.broadcasted_iota(jnp.int32, (1, 2 * half), 1)
    table, wide = [], []
    for pair, slips_ref in zip(pairs, slip_refs):
        for ref in pair:
            block = ref[k]
            turned = pltpu.roll(block.astype(jnp.float32), half, 1)
            table += [block, jnp.where(lane < half, turned, -turned).astype(jnp.bfloat16)]
        wide.append(jnp.concatenate([slips_ref[k, block] for block in range(slips_ref.shape[1])], axis=1))
    return lax.dot_general(
        jnp.concatenate(table, axis=0),
        jnp.concatenate(wide, axis=0),
        (((0,), (0,)), ((), ())),
        preferred_element_type=jnp.float32,
    )


def work_kernel(fills, sums, has_total, unroll, numbers_ref, *refs):
    refs = list(refs)
    take = lambda n: [refs.pop(0) for _ in range(n)]
    sources = take(4) if fills else None
    pairs, slip_refs = [], []
    for _ in range(sums):
        pairs.append(take(2))
        slip_refs += take(1)
    total_ref = take(1)[0] if has_total else None
    token = refs.pop()
    sum_ref = refs.pop() if sums else None
    outs = refs[len(refs) - len(fills) :]
    token[...] = jnp.zeros_like(token)

    def body(k, carry):
        if sums:
            term = sum_of(k, pairs, slip_refs)
            stations = term.shape[0] // 2
            for part in range(2):
                piece = term[part * stations : (part + 1) * stations]
                sum_ref[k, part] = piece + total_ref[k, part] if has_total else piece
        for unit, out in zip(fills, outs):
            fill(out, numbers_ref, unit, k, *sources)
        return carry

    lax.fori_loop(0, FREQS, body, 0, unroll=unroll)


FREQS = 16


def work(numbers, sources, fills, sums=(), total=None, after=(), unroll=2):
    columns, spots, own, other = sources
    variations = own.shape[1]
    args, aliases = [numbers], {}
    if fills:
        args += sources
    shapes = [
        jax.ShapeDtypeStruct((FREQS, variations // BLOCK, 4 * own.shape[0] // UNITS, BLOCK), jnp.bfloat16)
    ] * len(fills)
    for pair, unit_slips in sums:
        args += [*pair, unit_slips]
    if sums:
        if total is not None:
            aliases = {len(args): len(shapes)}
            args.append(total)
        shapes.append(jax.ShapeDtypeStruct((FREQS, 2, sums[0][0][0].shape[2] // 2, variations), jnp.float32))
    shapes.append(TOKEN)
    return pl.pallas_call(
        functools.partial(work_kernel, fills, len(sums), total is not None, unroll),
        out_shape=tuple(shapes),
        in_specs=[SMEM] + [VMEM] * (len(args) - 1) + [ANY] * len(after),
        out_specs=(VMEM,) * len(shapes),
        input_output_aliases=aliases,
        compiler_params=SMALL,
        cost_estimate=cost(3),
        name="fill" * len(fills) + "sum" * len(sums),
    )(*args, *after)


def finish_kernel(sums, unroll, rise_ref, *refs):
    pairs = [refs[3 * i : 3 * i + 2] for i in range(sums)]
    slip_refs = [refs[3 * i + 2] for i in range(sums)]
    total_ref = refs[3 * sums]
    out_ref, held, sems = refs[-3:]

    def copy(k):
        return pltpu.make_async_copy(held.at[k], out_ref.at[k], sems.at[k])

    def body(k, carry):
        term = sum_of(k, pairs, slip_refs)
        stations = term.shape[0] // 2
        re, im = term[:stations] + total_ref[k, 0], term[stations:] + total_ref[k, 1]
        pulsation = (k + 1).astype(jnp.float32) * (2.0 * jnp.pi * BASE_FREQ)
        damping = pulsation * rise_ref[...]
        scale = 1.0 / (1.0 + damping * damping)
        tilt = scale * damping
        held[k, 0] = scale * re + tilt * im
        held[k, 1] = scale * im - tilt * re
        copy(k).start()
        return carry

    lax.fori_loop(0, FREQS, body, 0, unroll=unroll)

    def drain(k, carry):
        copy(k).wait()
        return carry

    lax.fori_loop(0, FREQS, drain, 0)


def finish(rise_time, sums, total, unroll=4):
    args = [rise_time[None, :]]
    for pair, unit_slips in sums:
        args += [*pair, unit_slips]
    args.append(total)
    shape = jax.ShapeDtypeStruct(total.shape, jnp.float32)
    return pl.pallas_call(
        functools.partial(finish_kernel, len(sums), unroll),
        out_shape=(shape, shape),
        in_specs=[VMEM] * len(args),
        out_specs=(ANY, VMEM),
        scratch_shapes=[pltpu.SemaphoreType.DMA((FREQS,))],
        input_output_aliases={len(args) - 1: 1},
        compiler_params=SMALL,
        cost_estimate=cost(4),
        name="finish",
    )(*args)[0]


def swap(array, axis):
    return lax.ppermute(array, axis, [(0, 1), (1, 0)])


def exchange(piece, bits):
    return lax.ppermute(piece, "var", [(i, i ^ bits) for i in range(2 * UNITS)])


def gate_kernel(array_ref, token_ref, out_ref):
    pass


def gate(array, token):
    return pl.pallas_call(
        gate_kernel,
        out_shape=jax.ShapeDtypeStruct(array.shape, array.dtype),
        in_specs=[ANY, ANY],
        out_specs=ANY,
        input_output_aliases={0: 0},
        compiler_params=SMALL,
        name="gate",
    )(array, token)


def shards(size, fault_points, hypocenter, velocity, rise_time, member_mask, slip_amount, moment_tensor, strain_green, station_ids):
    freqs = strain_green.shape[4]
    half = moment_tensor.shape[1]
    rows = half // (2 * UNITS)
    swapped = [swap(array, "sub") for array in (member_mask, slip_amount)]
    own_part, other_part = rotate(strain_green[:, :, 0], moment_tensor, station_ids)
    received = swap(other_part, "sub")
    routed = size == 2 * UNITS
    if routed:
        place = lax.axis_index("var")
        block = jnp.concatenate([own_part, received], axis=1)
        pieces = [block, exchange(block, 2), exchange(block, 6)]
        numbers = jnp.stack([place % 2] + [(place // 2) ^ s for s in (0, 1, 3, 2)]).astype(jnp.int32)
    else:
        whole = [lax.all_gather(piece, "var", axis=1, tiled=True) for piece in (own_part, received)]
        pieces = [
            jnp.concatenate([part[:, i * rows : (i + 1) * rows] for part in whole], axis=1) for i in range(2 * UNITS)
        ]
        pairs = [(pieces[2 * i], pieces[2 * i + 1]) for i in range(UNITS)]
        numbers = jnp.arange(-1, UNITS, dtype=jnp.int32) * (jnp.arange(1 + UNITS, dtype=jnp.int32) > 0)

    own, other, columns, spots, token = prepare(
        fault_points, hypocenter, velocity, member_mask, slip_amount, *swapped, pieces[0]
    )
    step = functools.partial(work, numbers, (columns, spots, own, other))
    slips_0, token = step((0,), after=(token,))
    if routed:
        pieces[1] = gate(pieces[1], token)
        pairs = [(piece, exchange(piece, 1)) for piece in pieces[:2]]
    slips_1, token = step((1,), after=pieces[1:2])
    if routed:
        pieces[2] = gate(pieces[2], token)
        pairs.append((pieces[2], exchange(pieces[2], 1)))
        pairs.append((exchange(pieces[2], 2), exchange(pieces[2], 3)))
    slips_2, token = step((2,), after=pieces[2:3])
    slips_3, total, token = step((3,), ((pairs[0], slips_0), (pairs[1], slips_1)), after=(token,), unroll=8)
    return finish(rise_time, ((pairs[2], slips_2), (pairs[3], slips_3)), total, unroll=8)


def solution(mesh):
    placed = (
        P(None, "site"),
        P(("site", "var")),
        P(("site", "var")),
        P(("site", "var")),
        P(("site", "var"), "sub"),
        P(("site", "var"), "sub"),
        P(None, ("site", "sub")),
        P("site", None, "sub", "var", None, None),
        P("site"),
    )
    return jax.shard_map(
        functools.partial(shards, mesh.shape["var"]),
        mesh=mesh,
        in_specs=placed,
        out_specs=P(None, None, "sub", ("site", "var")),
        check_vma=False,
    )
```

```python
import functools

import jax
import jax.numpy as jnp
from jax import lax
from jax.experimental import pallas as pl
from jax.experimental.pallas import tpu as pltpu
from jax.sharding import PartitionSpec as P

VMEM = pl.BlockSpec(memory_space=pltpu.VMEM)
SMEM = pl.BlockSpec(memory_space=pltpu.SMEM)
ANY = pl.BlockSpec(memory_space=pl.ANY)
ROOMY = pltpu.CompilerParams(vmem_limit_bytes=56 * 2**20)
LARGE = pltpu.CompilerParams(vmem_limit_bytes=12 * 2**20)
SMALL = pltpu.CompilerParams(vmem_limit_bytes=4 * 2**20)
BASE_FREQ = 0.0625
LANES = 256
BLOCK = 128
UNITS = 4


def cost(microseconds):
    return pl.CostEstimate(flops=int(microseconds * 1.1e9), bytes_accessed=int(microseconds * 3e6), transcendentals=0)


def rotate_kernel(green_hbm, tensor_hbm, ids_hbm, own_ref, other_ref, green, tensor_ref, ids_ref, sums, rows, sems, few):
    _, comps, count, freqs, stations = green.shape
    half = stations // 2
    first = lax.axis_index("var") * count

    def load(part, comp):
        return pltpu.make_async_copy(green_hbm.at[part, comp], green.at[part, comp], sems.at[part, comp])

    small = [
        pltpu.make_async_copy(ids_hbm, ids_ref, few.at[0]),
        pltpu.make_async_copy(tensor_hbm, tensor_ref, few.at[1]),
    ]
    for copy in small:
        copy.start()
    for part in range(2):
        for comp in range(comps):
            load(part, comp).start()
    for copy in small:
        copy.wait()

    lane = lax.broadcasted_iota(jnp.int32, (1, stations), 1)
    ids = ids_ref[...]
    turned = pltpu.roll(ids, half, 1)
    low = jnp.where(lane < half, ids, turned)
    high = jnp.where(lane < half, turned, ids)
    is_first = lax.axis_index("sub") == 0
    wanted = jnp.concatenate([jnp.where(is_first, low, high), jnp.where(is_first, high, low)], axis=1)
    row = lax.broadcasted_iota(jnp.int32, (2 * stations, 2 * stations), 0)
    column = lax.broadcasted_iota(jnp.int32, (2 * stations, 2 * stations), 1)
    part_of_column = (column // half) % 2
    picks = (row == wanted + part_of_column * stations).astype(jnp.float32).astype(jnp.bfloat16)

    for part in range(2):
        for comp in range(comps):
            load(part, comp).wait()

        def one_subfault(m, carry, part=part):
            total = green[part, 0, m].astype(jnp.float32) * tensor_ref[0, first + m]
            for comp in range(1, comps):
                total = total + green[part, comp, m].astype(jnp.float32) * tensor_ref[comp, first + m]
            at = pl.ds(pl.multiple_of(m * freqs, freqs), freqs)
            sums[at, part * stations : (part + 1) * stations] = total.astype(jnp.bfloat16)
            return carry

        lax.fori_loop(0, count, one_subfault, 0, unroll=8)
    picked = jnp.dot(sums[...], picks, preferred_element_type=jnp.float32)
    rows[0] = picked[:, :stations]
    rows[1] = picked[:, stations:]
    for k in range(freqs):
        at = pl.ds(k, count, stride=freqs)
        own_ref[k] = rows[0, at, :].astype(jnp.bfloat16)
        other_ref[k] = rows[1, at, :].astype(jnp.bfloat16)


def rotate(green, tensor, station_ids):
    _, _, count, freqs, stations = green.shape
    piece = jax.ShapeDtypeStruct((freqs, count, stations), jnp.bfloat16)
    return pl.pallas_call(
        rotate_kernel,
        out_shape=(piece, piece),
        in_specs=[ANY] * 3,
        out_specs=(VMEM, VMEM),
        scratch_shapes=[
            pltpu.VMEM(green.shape, jnp.bfloat16),
            pltpu.SMEM(tensor.shape, jnp.float32),
            pltpu.VMEM((1, stations), jnp.int32),
            pltpu.VMEM((count * freqs, 2 * stations), jnp.bfloat16),
            pltpu.VMEM((2, count * freqs, stations), jnp.float32),
            pltpu.SemaphoreType.DMA(green.shape[:2]),
            pltpu.SemaphoreType.DMA((2,)),
        ],
        compiler_params=ROOMY,
        cost_estimate=cost(3),
        name="rotate",
    )(green, tensor, station_ids.reshape((1, stations)))


TOKEN = jax.ShapeDtypeStruct((8, 128), jnp.float32)


def prepare_kernel(
    points_ref, hypocenter_ref, velocity_ref, own_mask, own_slip, mask_hbm, slip_hbm, after_ref, *refs
):
    own_out, other_out, columns, spots, token, other_mask, other_slip, sems = refs
    half, variations = own_out.shape
    subfaults = 2 * half

    def load(i, part):
        rows = pl.ds(part * LANES, LANES)
        source, target = ((mask_hbm, other_mask), (slip_hbm, other_slip))[i]
        return pltpu.make_async_copy(source.at[rows], target.at[rows], sems.at[i, part])

    for part in range(variations // LANES):
        for i in range(2):
            load(i, part).start()
    token[...] = jnp.zeros_like(token)
    first = pl.multiple_of(lax.axis_index("sub") * half, half)
    second = pl.multiple_of(half - first, half)
    for axis in range(2):
        for at, start in ((0, first), (half, second)):
            wide = jnp.broadcast_to(points_ref[axis : axis + 1, pl.ds(start, half)], (BLOCK, half))
            columns[axis, at : at + half, :] = wide.T

    rest = points_ref[...]
    thirds = []
    for _ in range(3):
        thirds.append(rest.astype(jnp.bfloat16))
        rest = rest - thirds[-1].astype(jnp.float32)
    thirds = jnp.concatenate([t.astype(jnp.float32) for t in thirds], axis=0).astype(jnp.bfloat16)
    for lane in range(0, variations, LANES):
        lanes = slice(lane, lane + LANES)
        index = lax.broadcasted_iota(jnp.int32, (subfaults, LANES), 0)
        here = (index == hypocenter_ref[0:1, lanes]).astype(jnp.float32).astype(jnp.bfloat16)
        spot = jnp.dot(thirds, here, preferred_element_type=jnp.float32)
        spots[0:2, lanes] = (spot[0:2] + spot[2:4]) + spot[4:6]
        spots[2:3, lanes] = BASE_FREQ / velocity_ref[0:1, lanes]

    for mask, slip, out in ((own_mask, own_slip, own_out), (other_mask, other_slip, other_out)):
        for row in range(0, variations, BLOCK):
            if mask is other_mask and row % LANES == 0:
                load(0, row // LANES).wait()
                load(1, row // LANES).wait()
            rows = slice(row, row + BLOCK)
            out[:, rows] = (mask[rows, :].astype(jnp.float32) * slip[rows, :]).T


def prepare(points, hypocenter, velocity, own_mask, own_slip, other_mask, other_slip, after):
    variations, half = own_mask.shape
    out = jax.ShapeDtypeStruct((half, variations), jnp.float32)
    columns = jax.ShapeDtypeStruct((2, 2 * half, BLOCK), jnp.float32)
    spots = jax.ShapeDtypeStruct((8, variations), jnp.float32)
    return pl.pallas_call(
        prepare_kernel,
        out_shape=(out, out, columns, spots, TOKEN),
        in_specs=[VMEM] * 5 + [ANY] * 3,
        out_specs=(VMEM,) * 5,
        scratch_shapes=[
            pltpu.VMEM(other_mask.shape, jnp.int32),
            pltpu.VMEM(other_slip.shape, jnp.float32),
            pltpu.SemaphoreType.DMA((2, variations // LANES)),
        ],
        compiler_params=SMALL,
        cost_estimate=cost(3),
        name="prepare",
    )(points, hypocenter[None, :], velocity[None, :], own_mask, own_slip, other_mask, other_slip, after)


SIN = (3.14159264, -5.16771008, 2.55007751, -0.598291190, 0.0776574420)
COS = (0.999999953, -4.93479283, 4.05841131, -1.33187624, 0.219688854)


def sine_cosine(turns):
    rest = turns - jnp.floor(turns + 0.5)
    square = rest * rest
    sine = SIN[-1]
    for c in SIN[-2::-1]:
        sine = sine * square + c
    sine = sine * rest
    cosine = COS[-1]
    for c in COS[-2::-1]:
        cosine = cosine * square + c
    return 2.0 * sine * cosine, 1.0 - 2.0 * sine * sine


def fill(slips_ref, numbers_ref, unit, step, columns, spots, own_ref, other_ref):
    freqs, _, depth, _ = slips_ref.shape
    half = own_ref.shape[0]
    rows = depth // 8
    piece, block = step % 2, step // 2
    row = pl.multiple_of((2 * numbers_ref[1 + unit] + (piece ^ numbers_ref[0])) * rows, rows)
    lanes = pl.ds(pl.multiple_of(block * BLOCK, BLOCK), BLOCK)
    for part, source in enumerate((own_ref, other_ref)):
        at = pl.ds(part * half + row, rows)
        east = columns[0, at, :] - spots[0:1, lanes]
        north = columns[1, at, :] - spots[1:2, lanes]
        gap = east * east + north * north
        distance = gap * lax.rsqrt(jnp.maximum(gap, 1e-30))
        sine, cosine = sine_cosine(distance * spots[2:3, lanes])
        amount = source[pl.ds(row, rows), lanes]
        twice = 2.0 * cosine
        re_last, im_last = amount, None
        re, im = amount * cosine, amount * sine
        place = pl.multiple_of((4 * piece + part) * rows, rows)
        for k in range(freqs):
            slips_ref[k, block, pl.ds(place, rows), :] = re.astype(jnp.bfloat16)
            slips_ref[k, block, pl.ds(place + 2 * rows, rows), :] = im.astype(jnp.bfloat16)
            re, re_last = twice * re - re_last, re
            im, im_last = (twice * im if im_last is None else twice * im - im_last), im


def sum_of(k, pairs, slip_refs):
    half = pairs[0][0].shape[2] // 2
    lane = lax.broadcasted_iota(jnp.int32, (1, 2 * half), 1)
    table, wide = [], []
    for pair, slips_ref in zip(pairs, slip_refs):
        for ref in pair:
            block = ref[k]
            turned = pltpu.roll(block.astype(jnp.float32), half, 1)
            table += [block, jnp.where(lane < half, turned, -turned).astype(jnp.bfloat16)]
        wide.append(jnp.concatenate([slips_ref[k, block] for block in range(slips_ref.shape[1])], axis=1))
    return lax.dot_general(
        jnp.concatenate(table, axis=0),
        jnp.concatenate(wide, axis=0),
        (((0,), (0,)), ((), ())),
        preferred_element_type=jnp.float32,
    )


def late_fill_kernel(unit, numbers_ref, columns, spots, own_ref, other_ref, kept_ref, *refs):
    out_ref, token = refs[-2:]
    token[...] = jnp.zeros_like(token)

    @pl.when(numbers_ref[1 + UNITS] == 0)
    def _():
        def body(k, carry):
            fill(out_ref, numbers_ref, unit, k, columns, spots, own_ref, other_ref)
            return carry

        lax.fori_loop(0, FREQS, body, 0, unroll=4)


def late_fill(numbers, sources, unit, kept, after=()):
    args = [numbers, *sources, kept]
    return pl.pallas_call(
        functools.partial(late_fill_kernel, unit),
        out_shape=(jax.ShapeDtypeStruct(kept.shape, kept.dtype), TOKEN),
        in_specs=[SMEM] + [VMEM] * 5 + [ANY] * len(after),
        out_specs=(VMEM, VMEM),
        input_output_aliases={5: 0},
        compiler_params=SMALL,
        cost_estimate=cost(3),
        name="late_fill",
    )(*args, *after)


def work_kernel(fills, sums, has_total, unroll, guarded, numbers_ref, *refs):
    refs = list(refs)
    take = lambda n: [refs.pop(0) for _ in range(n)]
    sources = take(4) if fills else None
    pairs, slip_refs = [], []
    for _ in range(sums):
        pairs.append(take(2))
        slip_refs += take(1)
    total_ref = take(1)[0] if has_total else None
    token = refs.pop()
    sum_ref = refs.pop() if sums else None
    outs = refs[len(refs) - len(fills) :]
    token[...] = jnp.zeros_like(token)

    def body(k, carry):
        if sums:
            term = sum_of(k, pairs, slip_refs)
            stations = term.shape[0] // 2
            for part in range(2):
                piece = term[part * stations : (part + 1) * stations]
                sum_ref[k, part] = piece + total_ref[k, part] if has_total else piece
        for unit, out in zip(fills, outs):
            fill(out, numbers_ref, unit, k, *sources)
        return carry

    if guarded:
        for unit, out in zip(fills, outs):

            def only(k, carry, unit=unit, out=out):
                fill(out, numbers_ref, unit, k, *sources)
                return carry

            steps = FREQS if unit == fills[0] else numbers_ref[1 + UNITS] * FREQS // 2

            if unit == fills[0]:
                lax.fori_loop(0, FREQS, only, 0, unroll=unroll)
            else:
                lax.fori_loop(0, steps, lambda k, carry: only(2 * k + 1, only(2 * k, carry)), 0)
    else:
        lax.fori_loop(0, FREQS, body, 0, unroll=unroll)


FREQS = 16


def work(numbers, sources, fills, sums=(), total=None, after=(), unroll=4, guarded=False):
    columns, spots, own, other = sources
    variations = own.shape[1]
    args, aliases = [numbers], {}
    if fills:
        args += sources
    shapes = [
        jax.ShapeDtypeStruct((FREQS, variations // BLOCK, 4 * own.shape[0] // UNITS, BLOCK), jnp.bfloat16)
    ] * len(fills)
    for pair, unit_slips in sums:
        args += [*pair, unit_slips]
    if sums:
        if total is not None:
            aliases = {len(args): len(shapes)}
            args.append(total)
        shapes.append(jax.ShapeDtypeStruct((FREQS, 2, sums[0][0][0].shape[2] // 2, variations), jnp.float32))
    shapes.append(TOKEN)
    return pl.pallas_call(
        functools.partial(work_kernel, fills, len(sums), total is not None, unroll, guarded),
        out_shape=tuple(shapes),
        in_specs=[SMEM] + [VMEM] * (len(args) - 1) + [ANY] * len(after),
        out_specs=(VMEM,) * len(shapes),
        input_output_aliases=aliases,
        compiler_params=SMALL,
        cost_estimate=cost(3),
        name="fill" * len(fills) + "sum" * len(sums),
    )(*args, *after)


def finish_kernel(sums, unroll, rise_ref, *refs):
    pairs = [refs[3 * i : 3 * i + 2] for i in range(sums)]
    slip_refs = [refs[3 * i + 2] for i in range(sums)]
    total_ref = refs[3 * sums]
    out_ref, held, sems = refs[-3:]

    def copy(k):
        return pltpu.make_async_copy(held.at[k], out_ref.at[k], sems.at[k])

    def body(k, carry):
        term = sum_of(k, pairs, slip_refs)
        stations = term.shape[0] // 2
        re, im = term[:stations] + total_ref[k, 0], term[stations:] + total_ref[k, 1]
        pulsation = (k + 1).astype(jnp.float32) * (2.0 * jnp.pi * BASE_FREQ)
        damping = pulsation * rise_ref[...]
        scale = 1.0 / (1.0 + damping * damping)
        tilt = scale * damping
        held[k, 0] = scale * re + tilt * im
        held[k, 1] = scale * im - tilt * re
        copy(k).start()
        return carry

    lax.fori_loop(0, FREQS, body, 0, unroll=unroll)

    def drain(k, carry):
        copy(k).wait()
        return carry

    lax.fori_loop(0, FREQS, drain, 0)


def finish(rise_time, sums, total, unroll=4):
    args = [rise_time[None, :]]
    for pair, unit_slips in sums:
        args += [*pair, unit_slips]
    args.append(total)
    shape = jax.ShapeDtypeStruct(total.shape, jnp.float32)
    return pl.pallas_call(
        functools.partial(finish_kernel, len(sums), unroll),
        out_shape=shape,
        in_specs=[VMEM] * len(args),
        out_specs=ANY,
        scratch_shapes=[pltpu.VMEM(total.shape, jnp.float32), pltpu.SemaphoreType.DMA((FREQS,))],
        compiler_params=LARGE,
        cost_estimate=cost(4),
        name="finish",
    )(*args)


def swap(array, axis):
    return lax.ppermute(array, axis, [(0, 1), (1, 0)])


def exchange(piece, bits):
    return lax.ppermute(piece, "var", [(i, i ^ bits) for i in range(2 * UNITS)])


def gate_kernel(array_ref, token_ref, out_ref):
    pass


def gate(array, token):
    return pl.pallas_call(
        gate_kernel,
        out_shape=jax.ShapeDtypeStruct(array.shape, array.dtype),
        in_specs=[ANY, ANY],
        out_specs=ANY,
        input_output_aliases={0: 0},
        compiler_params=SMALL,
        name="gate",
    )(array, token)


def shards(size, fault_points, hypocenter, velocity, rise_time, member_mask, slip_amount, moment_tensor, strain_green, station_ids):
    freqs = strain_green.shape[4]
    half = moment_tensor.shape[1]
    rows = half // (2 * UNITS)
    swapped = [swap(array, "sub") for array in (member_mask, slip_amount)]
    own_part, other_part = rotate(strain_green[:, :, 0], moment_tensor, station_ids)
    received = swap(other_part, "sub")
    routed = size == 2 * UNITS
    if routed:
        place = lax.axis_index("var")
        block = jnp.concatenate([own_part, received], axis=1)
        pieces = [block, exchange(block, 2), exchange(block, 6)]
        early = place // 2 == UNITS - 1
        numbers = jnp.stack([place % 2] + [(place // 2) ^ s for s in (0, 1, 3, 2)] + [early]).astype(jnp.int32)
    else:
        whole = [lax.all_gather(piece, "var", axis=1, tiled=True) for piece in (own_part, received)]
        pieces = [
            jnp.concatenate([part[:, i * rows : (i + 1) * rows] for part in whole], axis=1) for i in range(2 * UNITS)
        ]
        pairs = [(pieces[2 * i], pieces[2 * i + 1]) for i in range(UNITS)]
        numbers = jnp.asarray([0, *range(UNITS), 0], jnp.int32)

    own, other, columns, spots, token = prepare(
        fault_points, hypocenter, velocity, member_mask, slip_amount, *swapped, pieces[0]
    )
    step = functools.partial(work, numbers, (columns, spots, own, other))
    slips_0, slips_1, token = step((0, 1), after=(token,), guarded=True)
    if routed:
        pieces[1] = gate(pieces[1], token)
        pairs = [(piece, exchange(piece, 1)) for piece in pieces[:2]]
    slips_1, token = late_fill(numbers, (columns, spots, own, other), 1, slips_1, after=pieces[1:2])
    if routed:
        pieces[2] = gate(pieces[2], token)
        pairs.append((pieces[2], exchange(pieces[2], 1)))
        pairs.append((exchange(pieces[2], 2), exchange(pieces[2], 3)))
    slips_2, token = step((2,), after=pieces[2:3])
    slips_3, total, token = step((3,), ((pairs[0], slips_0), (pairs[1], slips_1)), after=(token,), unroll=8)
    return finish(rise_time, ((pairs[2], slips_2), (pairs[3], slips_3)), total, unroll=8)


def solution(mesh):
    placed = (
        P(None, "site"),
        P(("site", "var")),
        P(("site", "var")),
        P(("site", "var")),
        P(("site", "var"), "sub"),
        P(("site", "var"), "sub"),
        P(None, ("site", "sub")),
        P("site", None, "sub", "var", None, None),
        P("site"),
    )
    return jax.shard_map(
        functools.partial(shards, mesh.shape["var"]),
        mesh=mesh,
        in_specs=placed,
        out_specs=P(None, None, "sub", ("site", "var")),
        check_vma=False,
    )
```

```python
import functools

import jax
import jax.numpy as jnp
from jax import lax
from jax.experimental import pallas as pl
from jax.experimental.pallas import tpu as pltpu
from jax.sharding import PartitionSpec as P

VMEM = pl.BlockSpec(memory_space=pltpu.VMEM)
SMEM = pl.BlockSpec(memory_space=pltpu.SMEM)
ANY = pl.BlockSpec(memory_space=pl.ANY)
ROOMY = pltpu.CompilerParams(vmem_limit_bytes=56 * 2**20)
LARGE = pltpu.CompilerParams(vmem_limit_bytes=12 * 2**20)
SMALL = pltpu.CompilerParams(vmem_limit_bytes=4 * 2**20)
BASE_FREQ = 0.0625
LANES = 256
BLOCK = 128
UNITS = 4


def cost(microseconds):
    return pl.CostEstimate(flops=int(microseconds * 1.1e9), bytes_accessed=int(microseconds * 3e6), transcendentals=0)


def rotate_kernel(green_hbm, tensor_hbm, ids_hbm, own_ref, other_ref, green, tensor_ref, ids_ref, sums, rows, sems, few):
    _, comps, count, freqs, stations = green.shape
    half = stations // 2
    first = lax.axis_index("var") * count

    def load(part, comp):
        return pltpu.make_async_copy(green_hbm.at[part, comp], green.at[part, comp], sems.at[part, comp])

    small = [
        pltpu.make_async_copy(ids_hbm, ids_ref, few.at[0]),
        pltpu.make_async_copy(tensor_hbm, tensor_ref, few.at[1]),
    ]
    for copy in small:
        copy.start()
    for part in range(2):
        for comp in range(comps):
            load(part, comp).start()
    for copy in small:
        copy.wait()

    lane = lax.broadcasted_iota(jnp.int32, (1, stations), 1)
    ids = ids_ref[...]
    turned = pltpu.roll(ids, half, 1)
    low = jnp.where(lane < half, ids, turned)
    high = jnp.where(lane < half, turned, ids)
    is_first = lax.axis_index("sub") == 0
    wanted = jnp.concatenate([jnp.where(is_first, low, high), jnp.where(is_first, high, low)], axis=1)
    row = lax.broadcasted_iota(jnp.int32, (2 * stations, 2 * stations), 0)
    column = lax.broadcasted_iota(jnp.int32, (2 * stations, 2 * stations), 1)
    part_of_column = (column // half) % 2
    picks = (row == wanted + part_of_column * stations).astype(jnp.float32).astype(jnp.bfloat16)

    for part in range(2):
        for comp in range(comps):
            load(part, comp).wait()

        def one_subfault(m, carry, part=part):
            total = green[part, 0, m].astype(jnp.float32) * tensor_ref[0, first + m]
            for comp in range(1, comps):
                total = total + green[part, comp, m].astype(jnp.float32) * tensor_ref[comp, first + m]
            at = pl.ds(pl.multiple_of(m * freqs, freqs), freqs)
            sums[at, part * stations : (part + 1) * stations] = total.astype(jnp.bfloat16)
            return carry

        lax.fori_loop(0, count, one_subfault, 0, unroll=8)
    picked = jnp.dot(sums[...], picks, preferred_element_type=jnp.float32)
    rows[0] = picked[:, :stations]
    rows[1] = picked[:, stations:]
    for k in range(freqs):
        at = pl.ds(k, count, stride=freqs)
        own_ref[k] = rows[0, at, :].astype(jnp.bfloat16)
        other_ref[k] = rows[1, at, :].astype(jnp.bfloat16)


def rotate(green, tensor, station_ids):
    _, _, count, freqs, stations = green.shape
    piece = pltpu.VMEM((freqs, count, stations), jnp.bfloat16)
    return pl.pallas_call(
        rotate_kernel,
        out_shape=(piece, piece),
        in_specs=[ANY] * 3,
        out_specs=(VMEM, VMEM),
        scratch_shapes=[
            pltpu.VMEM(green.shape, jnp.bfloat16),
            pltpu.SMEM(tensor.shape, jnp.float32),
            pltpu.VMEM((1, stations), jnp.int32),
            pltpu.VMEM((count * freqs, 2 * stations), jnp.bfloat16),
            pltpu.VMEM((2, count * freqs, stations), jnp.float32),
            pltpu.SemaphoreType.DMA(green.shape[:2]),
            pltpu.SemaphoreType.DMA((2,)),
        ],
        compiler_params=ROOMY,
        cost_estimate=cost(3),
        name="rotate",
    )(green, tensor, station_ids.reshape((1, stations)))


TOKEN = jax.ShapeDtypeStruct((8, 128), jnp.float32)


def prepare_kernel(
    points_ref, hypocenter_ref, velocity_ref, own_mask, own_slip, mask_hbm, slip_hbm, after_ref, *refs
):
    own_out, other_out, columns, spots, token, other_mask, other_slip, sems = refs
    half, variations = own_out.shape
    subfaults = 2 * half

    def load(i, part):
        rows = pl.ds(part * LANES, LANES)
        source, target = ((mask_hbm, other_mask), (slip_hbm, other_slip))[i]
        return pltpu.make_async_copy(source.at[rows], target.at[rows], sems.at[i, part])

    for part in range(variations // LANES):
        for i in range(2):
            load(i, part).start()
    token[...] = jnp.zeros_like(token)
    first = pl.multiple_of(lax.axis_index("sub") * half, half)
    second = pl.multiple_of(half - first, half)
    for axis in range(2):
        for at, start in ((0, first), (half, second)):
            wide = jnp.broadcast_to(points_ref[axis : axis + 1, pl.ds(start, half)], (BLOCK, half))
            columns[axis, at : at + half, :] = wide.T

    rest = points_ref[...]
    thirds = []
    for _ in range(3):
        thirds.append(rest.astype(jnp.bfloat16))
        rest = rest - thirds[-1].astype(jnp.float32)
    thirds = jnp.concatenate([t.astype(jnp.float32) for t in thirds], axis=0).astype(jnp.bfloat16)
    for lane in range(0, variations, LANES):
        lanes = slice(lane, lane + LANES)
        index = lax.broadcasted_iota(jnp.int32, (subfaults, LANES), 0)
        here = (index == hypocenter_ref[0:1, lanes]).astype(jnp.float32).astype(jnp.bfloat16)
        spot = jnp.dot(thirds, here, preferred_element_type=jnp.float32)
        spots[0:2, lanes] = (spot[0:2] + spot[2:4]) + spot[4:6]
        spots[2:3, lanes] = BASE_FREQ / velocity_ref[0:1, lanes]

    for mask, slip, out in ((own_mask, own_slip, own_out), (other_mask, other_slip, other_out)):
        for row in range(0, variations, BLOCK):
            if mask is other_mask and row % LANES == 0:
                load(0, row // LANES).wait()
                load(1, row // LANES).wait()
            rows = slice(row, row + BLOCK)
            out[:, rows] = (mask[rows, :].astype(jnp.float32) * slip[rows, :]).T


def prepare(points, hypocenter, velocity, own_mask, own_slip, other_mask, other_slip, after):
    variations, half = own_mask.shape
    out = jax.ShapeDtypeStruct((half, variations), jnp.float32)
    columns = jax.ShapeDtypeStruct((2, 2 * half, BLOCK), jnp.float32)
    spots = jax.ShapeDtypeStruct((8, variations), jnp.float32)
    return pl.pallas_call(
        prepare_kernel,
        out_shape=(out, out, columns, spots, TOKEN),
        in_specs=[VMEM] * 5 + [ANY] * 3,
        out_specs=(VMEM,) * 5,
        scratch_shapes=[
            pltpu.VMEM(other_mask.shape, jnp.int32),
            pltpu.VMEM(other_slip.shape, jnp.float32),
            pltpu.SemaphoreType.DMA((2, variations // LANES)),
        ],
        compiler_params=SMALL,
        cost_estimate=cost(3),
        name="prepare",
    )(points, hypocenter[None, :], velocity[None, :], own_mask, own_slip, other_mask, other_slip, after)


SIN = (3.14159264, -5.16771008, 2.55007751, -0.598291190, 0.0776574420)
COS = (0.999999953, -4.93479283, 4.05841131, -1.33187624, 0.219688854)


def sine_cosine(turns):
    rest = turns - jnp.floor(turns + 0.5)
    square = rest * rest
    sine = SIN[-1]
    for c in SIN[-2::-1]:
        sine = sine * square + c
    sine = sine * rest
    cosine = COS[-1]
    for c in COS[-2::-1]:
        cosine = cosine * square + c
    return 2.0 * sine * cosine, 1.0 - 2.0 * sine * sine


def fill(slips_ref, numbers_ref, unit, step, columns, spots, own_ref, other_ref):
    freqs, _, depth, _ = slips_ref.shape
    half = own_ref.shape[0]
    rows = depth // 8
    piece, block = step % 2, step // 2
    row = pl.multiple_of((2 * numbers_ref[1 + unit] + (piece ^ numbers_ref[0])) * rows, rows)
    lanes = pl.ds(pl.multiple_of(block * BLOCK, BLOCK), BLOCK)
    for part, source in enumerate((own_ref, other_ref)):
        at = pl.ds(part * half + row, rows)
        east = columns[0, at, :] - spots[0:1, lanes]
        north = columns[1, at, :] - spots[1:2, lanes]
        gap = east * east + north * north
        distance = gap * lax.rsqrt(jnp.maximum(gap, 1e-30))
        sine, cosine = sine_cosine(distance * spots[2:3, lanes])
        amount = source[pl.ds(row, rows), lanes]
        twice = 2.0 * cosine
        re_last, im_last = amount, None
        re, im = amount * cosine, amount * sine
        place = pl.multiple_of((4 * piece + part) * rows, rows)
        for k in range(freqs):
            slips_ref[k, block, pl.ds(place, rows), :] = re.astype(jnp.bfloat16)
            slips_ref[k, block, pl.ds(place + 2 * rows, rows), :] = im.astype(jnp.bfloat16)
            re, re_last = twice * re - re_last, re
            im, im_last = (twice * im if im_last is None else twice * im - im_last), im


def sum_of(k, pairs, slip_refs):
    half = pairs[0][0].shape[2] // 2
    lane = lax.broadcasted_iota(jnp.int32, (1, 2 * half), 1)
    table, wide = [], []
    for pair, slips_ref in zip(pairs, slip_refs):
        for ref in pair:
            block = ref[k]
            turned = pltpu.roll(block.astype(jnp.float32), half, 1)
            table += [block, jnp.where(lane < half, turned, -turned).astype(jnp.bfloat16)]
        wide.append(jnp.concatenate([slips_ref[k, block] for block in range(slips_ref.shape[1])], axis=1))
    return lax.dot_general(
        jnp.concatenate(table, axis=0),
        jnp.concatenate(wide, axis=0),
        (((0,), (0,)), ((), ())),
        preferred_element_type=jnp.float32,
    )


def late_fill_kernel(unit, numbers_ref, columns, spots, own_ref, other_ref, kept_ref, *refs):
    out_ref, token = refs[-2:]
    token[...] = jnp.zeros_like(token)

    @pl.when(numbers_ref[1 + UNITS] == 0)
    def _():
        def body(k, carry):
            fill(out_ref, numbers_ref, unit, k, columns, spots, own_ref, other_ref)
            return carry

        lax.fori_loop(0, FREQS, body, 0, unroll=4)


def late_fill(numbers, sources, unit, kept, after=()):
    args = [numbers, *sources, kept]
    return pl.pallas_call(
        functools.partial(late_fill_kernel, unit),
        out_shape=(jax.ShapeDtypeStruct(kept.shape, kept.dtype), TOKEN),
        in_specs=[SMEM] + [VMEM] * 5 + [ANY] * len(after),
        out_specs=(VMEM, VMEM),
        input_output_aliases={5: 0},
        compiler_params=SMALL,
        cost_estimate=cost(3),
        name="late_fill",
    )(*args, *after)


def work_kernel(fills, sums, has_total, unroll, guarded, numbers_ref, *refs):
    refs = list(refs)
    take = lambda n: [refs.pop(0) for _ in range(n)]
    sources = take(4) if fills else None
    pairs, slip_refs = [], []
    for _ in range(sums):
        pairs.append(take(2))
        slip_refs += take(1)
    total_ref = take(1)[0] if has_total else None
    token = refs.pop()
    sum_ref = refs.pop() if sums else None
    outs = refs[len(refs) - len(fills) :]
    token[...] = jnp.zeros_like(token)

    def body(k, carry):
        if sums:
            term = sum_of(k, pairs, slip_refs)
            stations = term.shape[0] // 2
            for part in range(2):
                piece = term[part * stations : (part + 1) * stations]
                sum_ref[k, part] = piece + total_ref[k, part] if has_total else piece
        for unit, out in zip(fills, outs):
            fill(out, numbers_ref, unit, k, *sources)
        return carry

    if guarded:
        for unit, out in zip(fills, outs):

            def only(k, carry, unit=unit, out=out):
                fill(out, numbers_ref, unit, k, *sources)
                return carry

            steps = FREQS if unit == fills[0] else numbers_ref[1 + UNITS] * FREQS // 2

            if unit == fills[0]:
                lax.fori_loop(0, FREQS, only, 0, unroll=unroll)
            else:
                lax.fori_loop(0, steps, lambda k, carry: only(2 * k + 1, only(2 * k, carry)), 0)
    else:
        lax.fori_loop(0, FREQS, body, 0, unroll=unroll)


FREQS = 16


def work(numbers, sources, fills, sums=(), total=None, after=(), unroll=4, guarded=False):
    columns, spots, own, other = sources
    variations = own.shape[1]
    args, aliases = [numbers], {}
    if fills:
        args += sources
    shapes = [
        jax.ShapeDtypeStruct((FREQS, variations // BLOCK, 4 * own.shape[0] // UNITS, BLOCK), jnp.bfloat16)
    ] * len(fills)
    for pair, unit_slips in sums:
        args += [*pair, unit_slips]
    if sums:
        if total is not None:
            aliases = {len(args): len(shapes)}
            args.append(total)
        shapes.append(jax.ShapeDtypeStruct((FREQS, 2, sums[0][0][0].shape[2] // 2, variations), jnp.float32))
    shapes.append(TOKEN)
    return pl.pallas_call(
        functools.partial(work_kernel, fills, len(sums), total is not None, unroll, guarded),
        out_shape=tuple(shapes),
        in_specs=[SMEM] + [VMEM] * (len(args) - 1) + [ANY] * len(after),
        out_specs=(VMEM,) * len(shapes),
        input_output_aliases=aliases,
        compiler_params=SMALL,
        cost_estimate=cost(3),
        name="fill" * len(fills) + "sum" * len(sums),
    )(*args, *after)


def finish_kernel(sums, unroll, rise_ref, *refs):
    pairs = [refs[3 * i : 3 * i + 2] for i in range(sums)]
    slip_refs = [refs[3 * i + 2] for i in range(sums)]
    total_ref = refs[3 * sums]
    out_ref, held, sems = refs[-3:]

    def copy(k):
        return pltpu.make_async_copy(held.at[k], out_ref.at[k], sems.at[k])

    def body(k, carry):
        term = sum_of(k, pairs, slip_refs)
        stations = term.shape[0] // 2
        re, im = term[:stations] + total_ref[k, 0], term[stations:] + total_ref[k, 1]
        pulsation = (k + 1).astype(jnp.float32) * (2.0 * jnp.pi * BASE_FREQ)
        damping = pulsation * rise_ref[...]
        scale = 1.0 / (1.0 + damping * damping)
        tilt = scale * damping
        held[k, 0] = scale * re + tilt * im
        held[k, 1] = scale * im - tilt * re
        copy(k).start()
        return carry

    lax.fori_loop(0, FREQS, body, 0, unroll=unroll)

    def drain(k, carry):
        copy(k).wait()
        return carry

    lax.fori_loop(0, FREQS, drain, 0)


def finish(rise_time, sums, total, unroll=4):
    args = [rise_time[None, :]]
    for pair, unit_slips in sums:
        args += [*pair, unit_slips]
    args.append(total)
    shape = jax.ShapeDtypeStruct(total.shape, jnp.float32)
    return pl.pallas_call(
        functools.partial(finish_kernel, len(sums), unroll),
        out_shape=shape,
        in_specs=[VMEM] * len(args),
        out_specs=ANY,
        scratch_shapes=[pltpu.VMEM(total.shape, jnp.float32), pltpu.SemaphoreType.DMA((FREQS,))],
        compiler_params=LARGE,
        cost_estimate=cost(4),
        name="finish",
    )(*args)


def swap(array, axis):
    return lax.ppermute(array, axis, [(0, 1), (1, 0)])


def exchange(piece, bits):
    return lax.ppermute(piece, "var", [(i, i ^ bits) for i in range(2 * UNITS)])


def gate_kernel(array_ref, token_ref, out_ref):
    pass


def gate(array, token):
    return pl.pallas_call(
        gate_kernel,
        out_shape=jax.ShapeDtypeStruct(array.shape, array.dtype),
        in_specs=[ANY, ANY],
        out_specs=ANY,
        input_output_aliases={0: 0},
        compiler_params=SMALL,
        name="gate",
    )(array, token)


def shards(size, fault_points, hypocenter, velocity, rise_time, member_mask, slip_amount, moment_tensor, strain_green, station_ids):
    freqs = strain_green.shape[4]
    half = moment_tensor.shape[1]
    rows = half // (2 * UNITS)
    swapped = [swap(array, "sub") for array in (member_mask, slip_amount)]
    own_part, other_part = rotate(strain_green[:, :, 0], moment_tensor, station_ids)
    received = swap(other_part, "sub")
    routed = size == 2 * UNITS
    if routed:
        place = lax.axis_index("var")
        block = jnp.concatenate([own_part, received], axis=1)
        pieces = [block, exchange(block, 2), exchange(block, 6)]
        early = place // 2 == UNITS - 1
        numbers = jnp.stack([place % 2] + [(place // 2) ^ s for s in (0, 1, 3, 2)] + [early]).astype(jnp.int32)
    else:
        whole = [lax.all_gather(piece, "var", axis=1, tiled=True) for piece in (own_part, received)]
        pieces = [
            jnp.concatenate([part[:, i * rows : (i + 1) * rows] for part in whole], axis=1) for i in range(2 * UNITS)
        ]
        pairs = [(pieces[2 * i], pieces[2 * i + 1]) for i in range(UNITS)]
        numbers = jnp.asarray([0, *range(UNITS), 0], jnp.int32)

    own, other, columns, spots, token = prepare(
        fault_points, hypocenter, velocity, member_mask, slip_amount, *swapped, pieces[0]
    )
    step = functools.partial(work, numbers, (columns, spots, own, other))
    slips_0, slips_1, token = step((0, 1), after=(token,), guarded=True)
    if routed:
        pieces[1] = gate(pieces[1], token)
        pairs = [(piece, exchange(piece, 1)) for piece in pieces[:2]]
    slips_1, token = late_fill(numbers, (columns, spots, own, other), 1, slips_1, after=pieces[1:2])
    if routed:
        pieces[2] = gate(pieces[2], token)
        pairs.append((pieces[2], exchange(pieces[2], 1)))
        pairs.append((exchange(pieces[2], 2), exchange(pieces[2], 3)))
    slips_2, token = step((2,), after=pieces[2:3])
    slips_3, total, token = step((3,), ((pairs[0], slips_0), (pairs[1], slips_1)), after=(token,), unroll=8)
    return finish(rise_time, ((pairs[2], slips_2), (pairs[3], slips_3)), total, unroll=8)


def solution(mesh):
    placed = (
        P(None, "site"),
        P(("site", "var")),
        P(("site", "var")),
        P(("site", "var")),
        P(("site", "var"), "sub"),
        P(("site", "var"), "sub"),
        P(None, ("site", "sub")),
        P("site", None, "sub", "var", None, None),
        P("site"),
    )
    return jax.shard_map(
        functools.partial(shards, mesh.shape["var"]),
        mesh=mesh,
        in_specs=placed,
        out_specs=P(None, None, "sub", ("site", "var")),
        check_vma=False,
    )
```

```python
import functools

import jax
import jax.numpy as jnp
from jax import lax
from jax.experimental import pallas as pl
from jax.experimental.pallas import tpu as pltpu
from jax.sharding import PartitionSpec as P

VMEM = pl.BlockSpec(memory_space=pltpu.VMEM)
SMEM = pl.BlockSpec(memory_space=pltpu.SMEM)
ANY = pl.BlockSpec(memory_space=pl.ANY)
ROOMY = pltpu.CompilerParams(vmem_limit_bytes=56 * 2**20)
LARGE = pltpu.CompilerParams(vmem_limit_bytes=12 * 2**20)
SMALL = pltpu.CompilerParams(vmem_limit_bytes=4 * 2**20)
BASE_FREQ = 0.0625
LANES = 256
BLOCK = 128
UNITS = 4


def cost(microseconds):
    return pl.CostEstimate(flops=int(microseconds * 1.1e9), bytes_accessed=int(microseconds * 3e6), transcendentals=0)


def rotate_kernel(green_hbm, tensor_hbm, ids_hbm, own_ref, other_ref, green, tensor_ref, ids_ref, sums, rows, sems, few):
    _, comps, count, freqs, stations = green.shape
    half = stations // 2
    first = lax.axis_index("var") * count

    def load(part, comp):
        return pltpu.make_async_copy(green_hbm.at[part, comp], green.at[part, comp], sems.at[part, comp])

    small = [
        pltpu.make_async_copy(ids_hbm, ids_ref, few.at[0]),
        pltpu.make_async_copy(tensor_hbm, tensor_ref, few.at[1]),
    ]
    for copy in small:
        copy.start()
    for part in range(2):
        for comp in range(comps):
            load(part, comp).start()
    for copy in small:
        copy.wait()

    lane = lax.broadcasted_iota(jnp.int32, (1, stations), 1)
    ids = ids_ref[...]
    turned = pltpu.roll(ids, half, 1)
    low = jnp.where(lane < half, ids, turned)
    high = jnp.where(lane < half, turned, ids)
    is_first = lax.axis_index("sub") == 0
    wanted = jnp.concatenate([jnp.where(is_first, low, high), jnp.where(is_first, high, low)], axis=1)
    row = lax.broadcasted_iota(jnp.int32, (2 * stations, 2 * stations), 0)
    column = lax.broadcasted_iota(jnp.int32, (2 * stations, 2 * stations), 1)
    part_of_column = (column // half) % 2
    picks = (row == wanted + part_of_column * stations).astype(jnp.float32).astype(jnp.bfloat16)

    for part in range(2):
        for comp in range(comps):
            load(part, comp).wait()

        def one_subfault(m, carry, part=part):
            total = green[part, 0, m].astype(jnp.float32) * tensor_ref[0, first + m]
            for comp in range(1, comps):
                total = total + green[part, comp, m].astype(jnp.float32) * tensor_ref[comp, first + m]
            at = pl.ds(pl.multiple_of(m * freqs, freqs), freqs)
            sums[at, part * stations : (part + 1) * stations] = total.astype(jnp.bfloat16)
            return carry

        lax.fori_loop(0, count, one_subfault, 0, unroll=8)
    picked = jnp.dot(sums[...], picks, preferred_element_type=jnp.float32)
    rows[0] = picked[:, :stations]
    rows[1] = picked[:, stations:]
    for k in range(freqs):
        at = pl.ds(k, count, stride=freqs)
        own_ref[k] = rows[0, at, :].astype(jnp.bfloat16)
        other_ref[k] = rows[1, at, :].astype(jnp.bfloat16)


def rotate(green, tensor, station_ids):
    _, _, count, freqs, stations = green.shape
    piece = pltpu.VMEM((freqs, count, stations), jnp.bfloat16)
    return pl.pallas_call(
        rotate_kernel,
        out_shape=(piece, piece),
        in_specs=[ANY] * 3,
        out_specs=(VMEM, VMEM),
        scratch_shapes=[
            pltpu.VMEM(green.shape, jnp.bfloat16),
            pltpu.SMEM(tensor.shape, jnp.float32),
            pltpu.VMEM((1, stations), jnp.int32),
            pltpu.VMEM((count * freqs, 2 * stations), jnp.bfloat16),
            pltpu.VMEM((2, count * freqs, stations), jnp.float32),
            pltpu.SemaphoreType.DMA(green.shape[:2]),
            pltpu.SemaphoreType.DMA((2,)),
        ],
        compiler_params=ROOMY,
        cost_estimate=cost(3),
        name="rotate",
    )(green, tensor, station_ids.reshape((1, stations)))


TOKEN = jax.ShapeDtypeStruct((8, 128), jnp.float32)


def prepare_kernel(
    points_ref, hypocenter_ref, velocity_ref, own_mask, own_slip, mask_hbm, slip_hbm, after_ref, *refs
):
    own_out, other_out, columns, spots, token, other_mask, other_slip, sems = refs
    half, variations = own_out.shape
    subfaults = 2 * half

    def load(i, part):
        rows = pl.ds(part * LANES, LANES)
        source, target = ((mask_hbm, other_mask), (slip_hbm, other_slip))[i]
        return pltpu.make_async_copy(source.at[rows], target.at[rows], sems.at[i, part])

    for part in range(variations // LANES):
        for i in range(2):
            load(i, part).start()
    token[...] = jnp.zeros_like(token)
    first = pl.multiple_of(lax.axis_index("sub") * half, half)
    second = pl.multiple_of(half - first, half)
    for axis in range(2):
        for at, start in ((0, first), (half, second)):
            wide = jnp.broadcast_to(points_ref[axis : axis + 1, pl.ds(start, half)], (BLOCK, half))
            columns[axis, at : at + half, :] = wide.T

    rest = points_ref[...]
    thirds = []
    for _ in range(3):
        thirds.append(rest.astype(jnp.bfloat16))
        rest = rest - thirds[-1].astype(jnp.float32)
    thirds = jnp.concatenate([t.astype(jnp.float32) for t in thirds], axis=0).astype(jnp.bfloat16)
    for lane in range(0, variations, LANES):
        lanes = slice(lane, lane + LANES)
        index = lax.broadcasted_iota(jnp.int32, (subfaults, LANES), 0)
        here = (index == hypocenter_ref[0:1, lanes]).astype(jnp.float32).astype(jnp.bfloat16)
        spot = jnp.dot(thirds, here, preferred_element_type=jnp.float32)
        spots[0:2, lanes] = (spot[0:2] + spot[2:4]) + spot[4:6]
        spots[2:3, lanes] = BASE_FREQ / velocity_ref[0:1, lanes]

    for mask, slip, out in ((own_mask, own_slip, own_out), (other_mask, other_slip, other_out)):
        for row in range(0, variations, BLOCK):
            if mask is other_mask and row % LANES == 0:
                load(0, row // LANES).wait()
                load(1, row // LANES).wait()
            rows = slice(row, row + BLOCK)
            out[:, rows] = (mask[rows, :].astype(jnp.float32) * slip[rows, :]).T


def prepare(points, hypocenter, velocity, own_mask, own_slip, other_mask, other_slip, after):
    variations, half = own_mask.shape
    out = jax.ShapeDtypeStruct((half, variations), jnp.float32)
    columns = jax.ShapeDtypeStruct((2, 2 * half, BLOCK), jnp.float32)
    spots = jax.ShapeDtypeStruct((8, variations), jnp.float32)
    return pl.pallas_call(
        prepare_kernel,
        out_shape=(out, out, columns, spots, TOKEN),
        in_specs=[VMEM] * 5 + [ANY] * 3,
        out_specs=(VMEM,) * 5,
        scratch_shapes=[
            pltpu.VMEM(other_mask.shape, jnp.int32),
            pltpu.VMEM(other_slip.shape, jnp.float32),
            pltpu.SemaphoreType.DMA((2, variations // LANES)),
        ],
        compiler_params=SMALL,
        cost_estimate=cost(3),
        name="prepare",
    )(points, hypocenter[None, :], velocity[None, :], own_mask, own_slip, other_mask, other_slip, after)


SIN = (3.14159264, -5.16771008, 2.55007751, -0.598291190, 0.0776574420)
COS = (0.999999953, -4.93479283, 4.05841131, -1.33187624, 0.219688854)


def sine_cosine(turns):
    rest = turns - jnp.floor(turns + 0.5)
    square = rest * rest
    sine = SIN[-1]
    for c in SIN[-2::-1]:
        sine = sine * square + c
    sine = sine * rest
    cosine = COS[-1]
    for c in COS[-2::-1]:
        cosine = cosine * square + c
    return 2.0 * sine * cosine, 1.0 - 2.0 * sine * sine


def fill(slips_ref, numbers_ref, unit, step, columns, spots, own_ref, other_ref):
    freqs, _, depth, _ = slips_ref.shape
    half = own_ref.shape[0]
    rows = depth // 8
    piece, block = step % 2, step // 2
    row = pl.multiple_of((2 * numbers_ref[1 + unit] + (piece ^ numbers_ref[0])) * rows, rows)
    lanes = pl.ds(pl.multiple_of(block * BLOCK, BLOCK), BLOCK)
    for part, source in enumerate((own_ref, other_ref)):
        at = pl.ds(part * half + row, rows)
        east = columns[0, at, :] - spots[0:1, lanes]
        north = columns[1, at, :] - spots[1:2, lanes]
        gap = east * east + north * north
        distance = gap * lax.rsqrt(jnp.maximum(gap, 1e-30))
        sine, cosine = sine_cosine(distance * spots[2:3, lanes])
        amount = source[pl.ds(row, rows), lanes]
        twice = 2.0 * cosine
        re_last, im_last = amount, None
        re, im = amount * cosine, amount * sine
        place = pl.multiple_of((4 * piece + part) * rows, rows)
        for k in range(freqs):
            slips_ref[k, block, pl.ds(place, rows), :] = re.astype(jnp.bfloat16)
            slips_ref[k, block, pl.ds(place + 2 * rows, rows), :] = im.astype(jnp.bfloat16)
            re, re_last = twice * re - re_last, re
            im, im_last = (twice * im if im_last is None else twice * im - im_last), im


def sum_of(k, pairs, slip_refs):
    half = pairs[0][0].shape[2] // 2
    lane = lax.broadcasted_iota(jnp.int32, (1, 2 * half), 1)
    table, wide = [], []
    for pair, slips_ref in zip(pairs, slip_refs):
        for ref in pair:
            block = ref[k]
            turned = pltpu.roll(block.astype(jnp.float32), half, 1)
            table += [block, jnp.where(lane < half, turned, -turned).astype(jnp.bfloat16)]
        wide.append(jnp.concatenate([slips_ref[k, block] for block in range(slips_ref.shape[1])], axis=1))
    return lax.dot_general(
        jnp.concatenate(table, axis=0),
        jnp.concatenate(wide, axis=0),
        (((0,), (0,)), ((), ())),
        preferred_element_type=jnp.float32,
    )


def late_fill_kernel(unit, numbers_ref, columns, spots, own_ref, other_ref, kept_ref, *refs):
    out_ref, token = refs[-2:]
    token[...] = jnp.zeros_like(token)

    @pl.when(numbers_ref[1 + UNITS] == 0)
    def _():
        def body(k, carry):
            fill(out_ref, numbers_ref, unit, k, columns, spots, own_ref, other_ref)
            return carry

        lax.fori_loop(0, FREQS, body, 0, unroll=4)


def late_fill(numbers, sources, unit, kept, after=()):
    args = [numbers, *sources, kept]
    return pl.pallas_call(
        functools.partial(late_fill_kernel, unit),
        out_shape=(jax.ShapeDtypeStruct(kept.shape, kept.dtype), TOKEN),
        in_specs=[SMEM] + [VMEM] * 5 + [ANY] * len(after),
        out_specs=(VMEM, VMEM),
        input_output_aliases={5: 0},
        compiler_params=SMALL,
        cost_estimate=cost(3),
        name="late_fill",
    )(*args, *after)


def work_kernel(fills, sums, has_total, unroll, guarded, numbers_ref, *refs):
    refs = list(refs)
    take = lambda n: [refs.pop(0) for _ in range(n)]
    sources = take(4) if fills else None
    pairs, slip_refs = [], []
    for _ in range(sums):
        pairs.append(take(2))
        slip_refs += take(1)
    total_ref = take(1)[0] if has_total else None
    token = refs.pop()
    sum_ref = refs.pop() if sums else None
    outs = refs[len(refs) - len(fills) :]
    token[...] = jnp.zeros_like(token)

    def body(k, carry):
        if sums:
            term = sum_of(k, pairs, slip_refs)
            stations = term.shape[0] // 2
            for part in range(2):
                piece = term[part * stations : (part + 1) * stations]
                sum_ref[k, part] = piece + total_ref[k, part] if has_total else piece
        for unit, out in zip(fills, outs):
            fill(out, numbers_ref, unit, k, *sources)
        return carry

    if guarded:
        for unit, out in zip(fills, outs):

            def only(k, carry, unit=unit, out=out):
                fill(out, numbers_ref, unit, k, *sources)
                return carry

            steps = FREQS if unit == fills[0] else numbers_ref[1 + UNITS] * FREQS // 2

            if unit == fills[0]:
                lax.fori_loop(0, FREQS, only, 0, unroll=unroll)
            else:
                lax.fori_loop(0, steps, lambda k, carry: only(2 * k + 1, only(2 * k, carry)), 0)
    else:
        lax.fori_loop(0, FREQS, body, 0, unroll=unroll)


FREQS = 16


def work(numbers, sources, fills, sums=(), total=None, after=(), unroll=4, guarded=False):
    columns, spots, own, other = sources
    variations = own.shape[1]
    args, aliases = [numbers], {}
    if fills:
        args += sources
    shapes = [
        jax.ShapeDtypeStruct((FREQS, variations // BLOCK, 4 * own.shape[0] // UNITS, BLOCK), jnp.bfloat16)
    ] * len(fills)
    for pair, unit_slips in sums:
        args += [*pair, unit_slips]
    if sums:
        if total is not None:
            aliases = {len(args): len(shapes)}
            args.append(total)
        shapes.append(jax.ShapeDtypeStruct((FREQS, 2, sums[0][0][0].shape[2] // 2, variations), jnp.float32))
    shapes.append(TOKEN)
    return pl.pallas_call(
        functools.partial(work_kernel, fills, len(sums), total is not None, unroll, guarded),
        out_shape=tuple(shapes),
        in_specs=[SMEM] + [VMEM] * (len(args) - 1) + [ANY] * len(after),
        out_specs=(VMEM,) * len(shapes),
        input_output_aliases=aliases,
        compiler_params=SMALL,
        cost_estimate=cost(3),
        name="fill" * len(fills) + "sum" * len(sums),
    )(*args, *after)


def finish_kernel(sums, unroll, rise_ref, *refs):
    pairs = [refs[3 * i : 3 * i + 2] for i in range(sums)]
    slip_refs = [refs[3 * i + 2] for i in range(sums)]
    total_ref = refs[3 * sums]
    out_ref, held, sems = refs[-3:]

    def copy(k):
        return pltpu.make_async_copy(held.at[k], out_ref.at[k], sems.at[k])

    def body(k, carry):
        term = sum_of(k, pairs, slip_refs)
        stations = term.shape[0] // 2
        re, im = term[:stations] + total_ref[k, 0], term[stations:] + total_ref[k, 1]
        pulsation = (k + 1).astype(jnp.float32) * (2.0 * jnp.pi * BASE_FREQ)
        damping = pulsation * rise_ref[...]
        scale = 1.0 / (1.0 + damping * damping)
        tilt = scale * damping
        held[k, 0] = scale * re + tilt * im
        held[k, 1] = scale * im - tilt * re
        copy(k).start()
        return carry

    lax.fori_loop(0, FREQS, body, 0, unroll=unroll)

    def drain(k, carry):
        copy(k).wait()
        return carry

    lax.fori_loop(0, FREQS, drain, 0)


def finish(rise_time, sums, total, unroll=4):
    args = [rise_time[None, :]]
    for pair, unit_slips in sums:
        args += [*pair, unit_slips]
    args.append(total)
    shape = jax.ShapeDtypeStruct(total.shape, jnp.float32)
    return pl.pallas_call(
        functools.partial(finish_kernel, len(sums), unroll),
        out_shape=shape,
        in_specs=[VMEM] * len(args),
        out_specs=ANY,
        scratch_shapes=[pltpu.VMEM(total.shape, jnp.float32), pltpu.SemaphoreType.DMA((FREQS,))],
        compiler_params=LARGE,
        cost_estimate=cost(4),
        name="finish",
    )(*args)


def swap(array, axis):
    return lax.ppermute(array, axis, [(0, 1), (1, 0)])


def exchange(piece, bits):
    return lax.ppermute(piece, "var", [(i, i ^ bits) for i in range(2 * UNITS)])


def gate_kernel(array_ref, token_ref, out_ref):
    pass


def gate(array, token):
    return pl.pallas_call(
        gate_kernel,
        out_shape=jax.ShapeDtypeStruct(array.shape, array.dtype),
        in_specs=[ANY, ANY],
        out_specs=ANY,
        input_output_aliases={0: 0},
        compiler_params=SMALL,
        name="gate",
    )(array, token)


def shards(size, fault_points, hypocenter, velocity, rise_time, member_mask, slip_amount, moment_tensor, strain_green, station_ids):
    freqs = strain_green.shape[4]
    half = moment_tensor.shape[1]
    rows = half // (2 * UNITS)
    swapped = [swap(array, "sub") for array in (member_mask, slip_amount)]
    own_part, other_part = rotate(strain_green[:, :, 0], moment_tensor, station_ids)
    received = swap(other_part, "sub")
    routed = size == 2 * UNITS
    if routed:
        place = lax.axis_index("var")
        block = jnp.concatenate([own_part, received], axis=1)
        pieces = [block, exchange(block, 2), exchange(block, 6)]
        early = place // 2 == UNITS - 1
        numbers = jnp.stack([place % 2] + [(place // 2) ^ s for s in (0, 1, 3, 2)] + [early]).astype(jnp.int32)
    else:
        whole = [lax.all_gather(piece, "var", axis=1, tiled=True) for piece in (own_part, received)]
        pieces = [
            jnp.concatenate([part[:, i * rows : (i + 1) * rows] for part in whole], axis=1) for i in range(2 * UNITS)
        ]
        pairs = [(pieces[2 * i], pieces[2 * i + 1]) for i in range(UNITS)]
        numbers = jnp.asarray([0, *range(UNITS), 0], jnp.int32)

    own, other, columns, spots, token = prepare(
        fault_points, hypocenter, velocity, member_mask, slip_amount, *swapped, pieces[0]
    )
    step = functools.partial(work, numbers, (columns, spots, own, other))
    slips_0, slips_1, token = step((0, 1), after=(token,), guarded=True)
    if routed:
        pieces[1] = gate(pieces[1], token)
        pairs = [(piece, exchange(piece, 1)) for piece in pieces[:2]]
    slips_1, token = late_fill(numbers, (columns, spots, own, other), 1, slips_1, after=pieces[1:2])
    if routed:
        pieces[2] = gate(pieces[2], token)
        pairs.append((pieces[2], exchange(pieces[2], 1)))
        pairs.append((exchange(pieces[2], 2), exchange(pieces[2], 3)))
    slips_2, token = step((2,), after=pieces[2:3])
    slips_3, total, token = step((3,), ((pairs[0], slips_0), (pairs[1], slips_1)), after=(token,), unroll=8)
    return finish(rise_time, ((pairs[2], slips_2), (pairs[3], slips_3)), total, unroll=16)


def solution(mesh):
    placed = (
        P(None, "site"),
        P(("site", "var")),
        P(("site", "var")),
        P(("site", "var")),
        P(("site", "var"), "sub"),
        P(("site", "var"), "sub"),
        P(None, ("site", "sub")),
        P("site", None, "sub", "var", None, None),
        P("site"),
    )
    return jax.shard_map(
        functools.partial(shards, mesh.shape["var"]),
        mesh=mesh,
        in_specs=placed,
        out_specs=P(None, None, "sub", ("site", "var")),
        check_vma=False,
    )
```
